32 devices in a mesh: dp: 2 (over y), mp: 16 (over z, x, core).
Axes of the slice: x: 2, y: 2, z: 4, core: 2. Of those that a mesh axis runs over, the one named last changes fastest.
Arguments:
- table_rows: bfloat16 [2, 16, 4608, 128], P('dp', 'mp'), may hold values from -6 to 6
- bag_ids: int32 [2, 16, 4608], P('dp', 'mp'), may hold values from 0 to 4095, never falling along the last dimension, each value on 1 to 8 neighbouring positions
- slot_feature: int32 [512], replicated, may hold values from 0 to 511, each once
- block_exponent: int32 [512, 4], replicated, may hold values from 0 to 3
- fm_project: bfloat16 [2, 512, 32], P(None, 'dp'), may hold values from -0.25 to 0.25
- fm_output: bfloat16 [2, 32, 128], P(None, 'dp'), may hold values from -0.09375 to 0.09375
- mix_weight: bfloat16 [2, 512, 512], P(None, 'dp'), may hold values from -0.25 to 0.25
- norm_gain: bfloat16 [2, 128], P(None, 'dp'), may hold values from 0.25 to 1.75
- out_cotangent: bfloat16 [256, 512, 128], P(('dp', 'mp')), may hold values from -6 to 6
Outputs:
- features_out: bfloat16 [256, 512, 128], P(('dp', 'mp'))
- row_grads: bfloat16 [2, 16, 4608, 128], P('dp', 'mp')
- grad_project: float32 [2, 512, 32], P(None, 'dp')
- grad_output: float32 [2, 32, 128], P(None, 'dp')
- grad_mix: float32 [2, 512, 512], P(None, 'dp')
- grad_gain: float32 [2, 128], P(None, 'dp')
The draws below stay inside these ranges and needn't reach their ends.
Inputs may be any that keep to these rules, and one draw needn't show every extreme that they name: `bag_ids`: on each device the bag numbers never fall along the rows; every one of the 4096 bags has 1 to 8 rows, some bag exactly 8. `slot_feature`: each feature stands in exactly one slot.
All inputs are finite; a program needn't handle non-finite values.
Results may differ from the reference program's by a relative error of at most 0.013.
Values may be sent and summed in bfloat16 or wider, within the bound.
No kernel may reach another device: no remote copies, remote signals or barrier semaphores. Data moves between devices by JAX's collectives and lax.ppermute only.
A program may use at most 64 MiB of HBM per device.

```python
import math
import jax
import jax.numpy as jnp
import numpy as np
from jax import lax

F = 512
E = 128
K = 32
LAYERS = 2
SAMP_DEV = 8
MAX_BAG = 8
BAGS = 4096
ROWS_DEV = 4608
SAMPLES = 256
BLOCKS = 4
N_DP = 2
N_MP = 16


def with_ends(values, stream_key, least, top_value):
    place = [jax.random.randint(jax.random.fold_in(stream_key, axis), (), 0, length) for axis, length in enumerate(values.shape)]
    longest = values.shape.index(max(values.shape))
    next_to = place[:longest] + [(place[longest] + 1) % values.shape[longest]] + place[longest + 1:]
    return values.at[tuple(place)].set(least).at[tuple(next_to)].set(top_value)


def block_scale(key, shape, shards, least, top_value):
    gain, own = 1.0, jax.random.fold_in(key, 6)
    for position, blocks in shards:
        heights = jnp.exp(jax.random.uniform(jax.random.fold_in(own, position), (blocks,), jnp.float32, least / len(shards), top_value / len(shards)))
        gain = gain * jnp.repeat(heights, shape[position] // blocks).reshape([-1 if axis == position else 1 for axis in range(len(shape))])
    return gain


def profile(amount, total, bound, skew):
    portions = [(1 << 20) // math.isqrt(grade ** skew) + 1 for grade in range(2, amount + 1)]
    surplus, counts = total - bound - (amount - 1), [1] * (amount - 1)
    while surplus > 0:
        free = [i for i in range(amount - 1) if counts[i] < bound]
        pool, left = sum([portions[i] for i in free]), surplus
        for i in free:
            extra = min(bound - counts[i], max(1, left * portions[i] // pool), surplus)
            counts[i] = counts[i] + extra
            surplus = surplus - extra
    return np.array([bound] + counts)


def uneven(own_key, amount, total, bound, slope):
    if amount == 2:
        one = jax.random.randint(own_key, (), max(1, total - bound), min(bound, total - 1) + 1)
        return jnp.stack([one, total - one])
    sizes = jnp.asarray(profile(amount, total, bound, slope), jnp.int32)
    couples = (amount - 1) // 2
    giver, sink = sizes[1:1 + 2 * couples:2], sizes[2:2 + 2 * couples:2]
    slack = jnp.minimum(giver - 1, bound - sink)
    moved = jax.random.randint(jax.random.fold_in(own_key, 1), (couples,), 0, 1 << 20) % (slack + 1)
    sizes = sizes.at[1:1 + 2 * couples:2].set(giver - moved).at[2:2 + 2 * couples:2].set(sink + moved)
    return sizes[jax.random.permutation(jax.random.fold_in(own_key, 2), amount)]


def gaussian(own_key, shape, scale, bound, pieces=(), kind=jnp.bfloat16):
    array = jax.random.normal(own_key, shape, jnp.float32) * scale
    if len(pieces) > 0:
        array = block_scale(own_key, shape, pieces, -0.22, 0.18) * array
    return jnp.clip(array, min=-bound, max=bound).astype(kind)


def setup_inputs(seed: int = 0) -> dict:
    arg_keys = jax.random.split(jax.random.key(seed), 10)
    return {
        "table_rows": gaussian(arg_keys[0], (N_DP, N_MP, ROWS_DEV, E), 1.0, 6.0, ((0, 2), (1, 16))),
        "bag_ids": jax.vmap(lambda own: jnp.searchsorted(jnp.cumsum(uneven(own, BAGS, ROWS_DEV, MAX_BAG, 2)), jnp.arange(ROWS_DEV), side="right"))(jax.random.split(arg_keys[1], N_DP * N_MP)).reshape((N_DP, N_MP, ROWS_DEV)).astype(jnp.int32),
        "slot_feature": jax.random.permutation(arg_keys[2], F).astype(jnp.int32),
        "block_exponent": with_ends(jax.random.randint(arg_keys[3], (F, BLOCKS), 0, 4), jax.random.fold_in(arg_keys[3], 1), 0, 3).astype(jnp.int32),
        "fm_project": gaussian(arg_keys[4], (LAYERS, F, K), F ** -0.5, 0.25, ((1, 2),)),
        "fm_output": gaussian(arg_keys[5], (LAYERS, K, E), (K * E) ** -0.5, 0.09375, ((1, 2),)),
        "mix_weight": gaussian(arg_keys[6], (LAYERS, F, F), F ** -0.5, 0.25, ((1, 2),)),
        "norm_gain": jnp.clip(1.0 + 0.15 * jax.random.normal(arg_keys[7], (LAYERS, E), jnp.float32), 0.25, 1.75).astype(jnp.bfloat16),
        "out_cotangent": gaussian(arg_keys[8], (SAMPLES, F, E), 1.0, 6.0, ((0, 32),)),
    }


EPS = 1e-05

def lowered(value):
    return lax.optimization_barrier(value.astype(jnp.bfloat16))

def product(form, left, right):
    return jnp.einsum(form, left.astype(jnp.float32), right.astype(jnp.float32))

def layer_forward(acts, project, output, mixing, gain_row):
    projected = lowered(product('sfe,fk->sek', acts, project))
    paired = lowered(product('sfe,sek->sfk', acts, projected))
    total = acts.astype(jnp.float32) + product('sfk,ke->sfe', paired, output) + product('gf,sfe->sge', mixing, acts)
    centred = total - lax.optimization_barrier(jnp.mean(total, axis=-1, keepdims=True))
    inverse_std = lax.rsqrt(lax.optimization_barrier(jnp.mean(centred * centred, axis=-1, keepdims=True)) + EPS)
    normed = centred * inverse_std
    result = lowered(normed * gain_row.astype(jnp.float32))
    return (result, (projected, paired, normed, inverse_std))

def layer_backward(upstream, acts, project, output, mixing, gain_row, saved):
    projected, paired, normed, inverse_std = saved
    upper = upstream.astype(jnp.float32)
    grad_gain = lax.optimization_barrier(jnp.sum(upper * normed, axis=(0, 1)))
    scaled = upper * gain_row.astype(jnp.float32)
    grad_total = inverse_std * (scaled - lax.optimization_barrier(jnp.mean(scaled, axis=-1, keepdims=True)) - normed * lax.optimization_barrier(jnp.mean(scaled * normed, axis=-1, keepdims=True)))
    total_low = lowered(grad_total)
    grad_output = product('sfk,sfe->ke', paired, total_low)
    grad_paired = lowered(product('sfe,ke->sfk', total_low, output))
    grad_mixing = product('sge,sfe->gf', total_low, acts)
    grad_projected = lowered(product('sfk,sfe->sek', grad_paired, acts))
    grad_project = product('sfe,sek->fk', acts, grad_projected)
    grad_acts = grad_total + product('gf,sge->sfe', mixing, total_low) + product('sfk,sek->sfe', grad_paired, projected) + product('fk,sek->sfe', project, grad_projected)
    return (lowered(grad_acts), (grad_project, grad_output, grad_mixing, grad_gain))

def reference(table_rows, bag_ids, slot_feature, block_exponent, fm_project, fm_output, mix_weight, norm_gain, out_cotangent):
    f_dev = F // N_MP
    group = SAMP_DEV * N_MP
    flat_rows = table_rows.reshape(N_DP * N_MP, ROWS_DEV, E)
    flat_ids = bag_ids.reshape(N_DP * N_MP, ROWS_DEV)

    def pool_one(rows_one, ids_one):
        return jax.ops.segment_sum(rows_one.astype(jnp.float32), ids_one, num_segments=BAGS, indices_are_sorted=True).astype(jnp.bfloat16)
    pooled = jax.vmap(pool_one)(flat_rows, flat_ids)
    slot_acts = pooled.reshape(N_DP, N_MP, group, f_dev, E).transpose(0, 2, 1, 3, 4).reshape(SAMPLES, F, E)
    inverse = jnp.zeros((F,), jnp.int32).at[slot_feature].set(jnp.arange(F, dtype=jnp.int32))
    scales = jnp.repeat(jnp.exp2((block_exponent - 2).astype(jnp.float32)), 32, axis=1)
    acts_zero = (slot_acts[:, inverse, :].astype(jnp.float32) * scales[None]).astype(jnp.bfloat16)

    def group_step(totals, inputs):
        acts, cotangent = inputs
        saved_all = []
        for layer in range(LAYERS):
            before = acts
            acts, saved = layer_forward(acts, fm_project[layer], fm_output[layer], mix_weight[layer], norm_gain[layer])
            saved_all.append((before, saved))
        final = acts
        upstream = cotangent
        collected = []
        for layer in reversed(range(LAYERS)):
            before, saved = saved_all[layer]
            upstream, grads = layer_backward(upstream, before, fm_project[layer], fm_output[layer], mix_weight[layer], norm_gain[layer], saved)
            collected.append(grads)
        collected = collected[::-1]
        stacked = tuple((jnp.stack([entry[index] for entry in collected]) for index in range(4)))
        totals = tuple((old + new for old, new in zip(totals, stacked)))
        return (totals, (final, upstream))
    start = (jnp.zeros((LAYERS, F, K), jnp.float32), jnp.zeros((LAYERS, K, E), jnp.float32), jnp.zeros((LAYERS, F, F), jnp.float32), jnp.zeros((LAYERS, E), jnp.float32))
    blocks_in = (acts_zero.reshape(N_DP, group, F, E), out_cotangent.reshape(N_DP, group, F, E))
    totals, (finals, upstreams) = lax.scan(group_step, start, blocks_in)
    features_out = finals.reshape(SAMPLES, F, E)
    upstream_zero = upstreams.reshape(SAMPLES, F, E)
    slot_grads = (upstream_zero[:, slot_feature, :].astype(jnp.float32) * scales[slot_feature][None]).astype(jnp.bfloat16)
    owner_grads = slot_grads.reshape(N_DP, group, N_MP, f_dev, E).transpose(0, 2, 1, 3, 4).reshape(N_DP * N_MP, BAGS, E)
    row_grads = jax.vmap(lambda grads_one, ids_one: grads_one[ids_one])(owner_grads, flat_ids).reshape(N_DP, N_MP, ROWS_DEV, E)
    factor = 1.0 / jnp.sqrt(jnp.float32(SAMPLES))
    return (features_out, row_grads, totals[0] * factor, totals[1] * factor, totals[2] * factor, totals[3] * factor)
```

```python
import functools

import jax
import jax.numpy as jnp
from jax import lax
from jax.experimental import pallas as pl
from jax.experimental.pallas import tpu as pltpu
from jax.sharding import PartitionSpec as P

F = 512
E = 128
K = 32
LAYERS = 2
SAMP_DEV = 8
PAIR = 2
PW = PAIR * E
EPS = 1e-05
VMEM_LIMIT = 56 * 1024 * 1024
PIECE = 144
BF = jnp.bfloat16
F32 = jnp.float32


def params():
    return pltpu.CompilerParams(vmem_limit_bytes=VMEM_LIMIT)


def dot(left, right):
    return jnp.dot(left, right, preferred_element_type=F32)


def dot_nt(left, right):
    return lax.dot_general(left, right, (((1,), (1,)), ((), ())), preferred_element_type=F32)


def dot_tn(left, right):
    return lax.dot_general(left, right, (((0,), (0,)), ((), ())), preferred_element_type=F32)


def pool_kernel(ids_ref, rows_ref, out_ref, *, block):
    bags, rows = out_ref.shape[0], rows_ref.shape[0]
    for low in range(0, bags, block):
        high = min(low + block + rows - bags, rows)
        bag = lax.broadcasted_iota(jnp.int32, (block, high - low), 0) + low
        hot = jnp.where(ids_ref[:, low:high] == bag, 1.0, 0.0).astype(BF)
        out_ref[low : low + block, :] = dot(hot, rows_ref[low:high, :]).astype(BF)


def pool(ids, rows, bags):
    return pl.pallas_call(
        functools.partial(pool_kernel, block=256),
        out_shape=jax.ShapeDtypeStruct((bags, E), BF),
        compiler_params=params(),
        name="pool",
    )(ids, rows)


def expand_kernel(ids_ref, bags_ref, out_ref, table, *, block):
    rows, bags = out_ref.shape[0], bags_ref.shape[0]
    table[...] = jnp.zeros_like(table)
    for part in range(rows // 128):
        table[part : part + 1, :] = ids_ref[:, part * 128 : (part + 1) * 128]
    columns = table[...].T
    for low in range(0, rows, block):
        first = max(low - (rows - bags), 0)
        last = min(low + block, bags)
        own = jnp.concatenate(
            [columns[:, part : part + 1] for part in range(low // 128, (low + block) // 128)], axis=0
        )
        bag = lax.broadcasted_iota(jnp.int32, (block, last - first), 1) + first
        hot = jnp.where(own == bag, 1.0, 0.0).astype(BF)
        out_ref[low : low + block, :] = dot(hot, bags_ref[first:last, :]).astype(BF)


def expand(ids, owner, rows):
    return pl.pallas_call(
        functools.partial(expand_kernel, block=256),
        out_shape=jax.ShapeDtypeStruct((rows, E), BF),
        scratch_shapes=[pltpu.VMEM((128, 128), jnp.int32)],
        compiler_params=params(),
        name="expand",
    )(ids, owner)


def prepare_kernel(
    slot_ref, expo_ref, project_ref, output_ref, mix_ref, left_ref, back_ref, diag_ref, scale_ref, perm_ref, unperm_ref
):
    for layer in range(LAYERS):
        left_ref[layer, :F, :] = mix_ref[layer]
        left_ref[layer, F:, :] = project_ref[layer].T
        back_ref[layer] = mix_ref[layer].T
        row = output_ref[layer]
        none = jnp.zeros_like(row)
        diag_ref[layer] = jnp.concatenate(
            [jnp.concatenate([row, none], axis=1), jnp.concatenate([none, row], axis=1)], axis=0
        )
    expo = expo_ref[...]
    small = jnp.where(
        expo == 0, 0.25, jnp.where(expo == 1, 0.5, jnp.where(expo == 2, 1.0, 2.0))
    ).astype(BF)
    blocks = expo.shape[1]
    spread = jnp.where(
        lax.broadcasted_iota(jnp.int32, (blocks, E), 1) // (E // blocks)
        == lax.broadcasted_iota(jnp.int32, (blocks, E), 0),
        1.0,
        0.0,
    ).astype(BF)
    scale_ref[...] = dot(small, spread)
    hot = jnp.where(slot_ref[...] == lax.broadcasted_iota(jnp.int32, (F, F), 0), 1.0, 0.0)
    perm_ref[...] = hot.astype(BF)
    unperm_ref[...] = hot.T.astype(BF)


def prepare(slot_feature, block_exponent, project, output, mix):
    return pl.pallas_call(
        prepare_kernel,
        out_shape=(
            jax.ShapeDtypeStruct((LAYERS, F + K, F), BF),
            jax.ShapeDtypeStruct((LAYERS, F, F), BF),
            jax.ShapeDtypeStruct((LAYERS, PAIR * K, PW), BF),
            jax.ShapeDtypeStruct((F, E), F32),
            jax.ShapeDtypeStruct((F, F), BF),
            jax.ShapeDtypeStruct((F, F), BF),
        ),
        compiler_params=params(),
        name="prepare",
    )(slot_feature.reshape(1, F), block_exponent, project, output, mix)


def unslot(block, f_dev):
    if f_dev % 16:
        block = block.astype(F32)
    parts = [block[:, t * f_dev : (t + 1) * f_dev, :].reshape(F, E) for t in range(PAIR)]
    return jnp.concatenate(parts, axis=1).astype(BF)


def layers_kernel(
    pos_ref,
    recv_ref,
    cot_ref,
    left_ref,
    back_ref,
    diag_ref,
    project_ref,
    gain_ref,
    scale_ref,
    perm_ref,
    unperm_ref,
    *refs,
    f_dev,
    packed,
):
    feats_ref, slots_ref = refs[:2]
    grad_refs = refs[2:4] if packed else refs[2:6]
    xs, ts, normed_s, inv_s, grad_s, next_s, wacc, gacc, dm, pj, ex = refs[-11:]
    step = pl.program_id(0)
    columns = pl.ds(pl.multiple_of(step * PW, PW), PW)
    scale = scale_ref[...]
    chunk = 128

    @pl.when(step == 0)
    def _():
        wacc[...] = jnp.zeros_like(wacc)
        gacc[...] = jnp.zeros_like(gacc)

    x = dot(perm_ref[...], unslot(recv_ref[...], f_dev))
    x = (x * jnp.concatenate([scale] * PAIR, axis=1)).astype(BF)
    same = (
        lax.broadcasted_iota(jnp.int32, (PAIR * K, PW), 0) // K
        == lax.broadcasted_iota(jnp.int32, (PAIR * K, PW), 1) // E
    )
    saved = []
    for layer in range(LAYERS):
        xs[layer, :, columns] = x
        mixed = dot(left_ref[layer], x)
        projected = jnp.concatenate([mixed[F:]] * PAIR, axis=0)
        projected = jnp.where(same, projected, 0.0).astype(BF)
        paired = dot_nt(x, projected).astype(BF)
        low = dot(paired, diag_ref[layer])
        gain = gain_ref[layer : layer + 1, :].astype(F32)
        saved.append((x, projected, paired))
        for t in range(PAIR):
            lanes = slice(t * E, (t + 1) * E)
            for r in range(0, F, chunk):
                rows = slice(r, r + chunk)
                total = x[rows, lanes].astype(F32) + mixed[rows, lanes] + low[rows, lanes]
                centred = total - jnp.sum(total, axis=-1, keepdims=True) * (1.0 / E)
                variance = jnp.sum(centred * centred, axis=-1, keepdims=True) * (1.0 / E)
                inverse = lax.rsqrt(variance + EPS)
                normed = centred * inverse
                normed_s[layer, rows, lanes] = normed
                inv_s[layer, rows, lanes] = jnp.broadcast_to(inverse, (chunk, E))
                out = (normed * gain).astype(BF)
                next_s[rows, lanes] = out
                if layer == LAYERS - 1:
                    feats_ref[t, rows, :] = out
        x = next_s[...]

    for layer in reversed(range(LAYERS)):
        x, projected, paired = saved[layer]
        gain = gain_ref[layer : layer + 1, :].astype(F32)
        dgain = jnp.zeros((8, E), F32)
        for t in range(PAIR):
            lanes = slice(t * E, (t + 1) * E)
            for r in range(0, F, chunk):
                rows = slice(r, r + chunk)
                if layer == LAYERS - 1:
                    upper = cot_ref[t, rows, :].astype(F32)
                else:
                    upper = next_s[rows, lanes].astype(F32)
                normed = normed_s[layer, rows, lanes]
                dgain = dgain + jnp.sum((upper * normed).reshape(chunk // 8, 8, E), axis=0)
                scaled = upper * gain
                first = jnp.sum(scaled, axis=-1, keepdims=True) * (1.0 / E)
                second = jnp.sum(scaled * normed, axis=-1, keepdims=True) * (1.0 / E)
                total = inv_s[layer, rows, lanes] * (scaled - first - normed * second)
                grad_s[rows, lanes] = total
                next_s[rows, lanes] = total.astype(BF)
        gacc[layer] += dgain
        total_low = next_s[...]
        ts[layer, :F, columns] = total_low
        grad_paired = dot_nt(total_low, diag_ref[layer]).astype(BF)
        wide = dot_tn(grad_paired, x)
        grad_projected = jnp.concatenate(
            [wide[t * K : (t + 1) * K, t * E : (t + 1) * E] for t in range(PAIR)], axis=1
        ).astype(BF)
        ts[layer, F:, columns] = grad_projected
        wide = dot_tn(paired, total_low)
        for t in range(PAIR):
            wacc[layer] += wide[t * K : (t + 1) * K, t * E : (t + 1) * E]
        upstream = dot(back_ref[layer], total_low) + dot(
            jnp.concatenate([grad_paired, project_ref[layer]], axis=1),
            jnp.concatenate([projected, grad_projected], axis=0),
        )
        for t in range(PAIR):
            lanes = slice(t * E, (t + 1) * E)
            for r in range(0, F, chunk):
                rows = slice(r, r + chunk)
                out = (grad_s[rows, lanes] + upstream[rows, lanes]).astype(BF)
                if layer == 0:
                    out = (out.astype(F32) * scale[rows]).astype(BF)
                next_s[rows, lanes] = out

    slots = dot(unperm_ref[...], next_s[...])
    if f_dev % 16 == 0:
        slots = slots.astype(BF)
    for t in range(PAIR):
        slots_ref[:, t * f_dev : (t + 1) * f_dev, :] = (
            slots[:, t * E : (t + 1) * E].reshape(F // f_dev, f_dev, E).astype(BF)
        )

    @pl.when(step == pl.num_programs(0) - 1)
    def _():
        for layer in range(LAYERS):
            dm[layer] = dot_nt(ts[layer], xs[layer])
        gains = [jnp.sum(gacc[layer], axis=0, keepdims=True) for layer in range(LAYERS)]
        if not packed:
            mix_ref, project_t_ref, output_ref, gain_out_ref = grad_refs
            mix_ref[...] = dm[:, :F, :]
            project_t_ref[...] = dm[:, F:, :]
            output_ref[...] = wacc[...]
            gain_out_ref[...] = jnp.concatenate(gains, axis=0)
            return
        half = F // 2
        for d in range(2):
            gain_row = jnp.concatenate([g[:, d * 64 : (d + 1) * 64] for g in gains], axis=1)
            for m in range(16):
                l, h, kb = m // 8, (m // 4) % 2, m % 4
                low = d * half + h * E
                pj[d, m] = dm[l, F + 8 * kb : F + 8 * kb + 8, low : low + E]
                if m < 4:
                    low = d * (K // 2) + 8 * (m % 2)
                    ex[d, m] = wacc[m // 2, low : low + 8, :]
                else:
                    ex[d, m] = jnp.broadcast_to(gain_row, (8, E))
        my_d, my_m = pos_ref[0], pos_ref[1]
        for core in range(2):
            for rx in range(2):
                for ry in range(2):
                    for rz in range(4):
                        m = my_m ^ (rz * 4 + rx * 2 + core)
                        d = my_d ^ ry
                        start = pl.multiple_of(d * half + (m % 8) * 32, 32)
                        block = dm[m // 8, pl.ds(start, 32), :]
                        pieces = [block[:, c * E : (c + 1) * E] for c in range(4)]
                        pieces += [pj[d, m], ex[d, m]]
                        grad_refs[core][(rx * 2 + ry) * 4 + rz] = jnp.concatenate(
                            pieces, axis=0
                        ).astype(BF)


def run_layers(pos, recv, cotangent, operands, project, gain, f_dev, packed):
    left, back, diag, scale, perm, unperm = operands
    tables = F // f_dev

    def whole(x):
        return pl.BlockSpec(x.shape, lambda i, pos: (0,) * x.ndim)

    def shape(dims, dtype=F32):
        return jax.ShapeDtypeStruct(dims, dtype)

    if packed:
        grads = [shape((16, PIECE, E), BF)] * 2
    else:
        grads = [
            shape((LAYERS, F, F)),
            shape((LAYERS, K, F)),
            shape((LAYERS, K, E)),
            shape((LAYERS, E)),
        ]
    cot_spec = pl.BlockSpec((PAIR, F, E), lambda i, pos: (i, 0, 0))
    slot_spec = pl.BlockSpec((tables, PAIR * f_dev, E), lambda i, pos: (0, i, 0))
    constants = [left, back, diag, project, gain, scale, perm, unperm]
    width = SAMP_DEV * E
    return pl.pallas_call(
        functools.partial(layers_kernel, f_dev=f_dev, packed=packed),
        out_shape=[
            shape((SAMP_DEV, F, E), BF),
            shape((tables, SAMP_DEV * f_dev, E), BF),
        ]
        + grads,
        grid_spec=pltpu.PrefetchScalarGridSpec(
            num_scalar_prefetch=1,
            grid=(SAMP_DEV // PAIR,),
            in_specs=[slot_spec, cot_spec] + [whole(x) for x in constants],
            out_specs=[cot_spec, slot_spec] + [whole(x) for x in grads],
            scratch_shapes=[
                pltpu.VMEM((LAYERS, F, width), BF),
                pltpu.VMEM((LAYERS, F + K, width), BF),
                pltpu.VMEM((LAYERS, F, PW), F32),
                pltpu.VMEM((LAYERS, F, PW), F32),
                pltpu.VMEM((F, PW), F32),
                pltpu.VMEM((F, PW), BF),
                pltpu.VMEM((LAYERS, K, E), F32),
                pltpu.VMEM((LAYERS, 8, E), F32),
                pltpu.VMEM((LAYERS, F + K, F), F32),
                pltpu.VMEM((2, 16, 8, E), F32),
                pltpu.VMEM((2, 16, 8, E), F32),
            ],
        ),
        compiler_params=params(),
        name="layers",
    )(pos, recv, cotangent, *constants)


def gather_dp(part, axis):
    if lax.axis_size("dp") != 2:
        return lax.all_gather(part, "dp", axis=axis, tiled=True)
    other = lax.ppermute(part, "dp", [(0, 1), (1, 0)])
    return jnp.where(
        lax.axis_index("dp") == 0,
        jnp.concatenate([part, other], axis=axis),
        jnp.concatenate([other, part], axis=axis),
    )


def across(x, d, m):
    pairs = [(i, i ^ (d * 16 + m)) for i in range(32)]
    return lax.ppermute(x, ("dp", "mp"), pairs)


def sum_kernel(*refs, parts):
    total = sum(ref[...].astype(F32) for ref in refs[:parts]).astype(BF)
    outs = refs[parts:]
    size = total.shape[0] // len(outs)
    for i, out in enumerate(outs):
        out[...] = total[i * size : (i + 1) * size]


def sum_parts(parts, outs):
    size = parts[0].shape[0] // outs
    return pl.pallas_call(
        functools.partial(sum_kernel, parts=len(parts)),
        out_shape=[jax.ShapeDtypeStruct((size,) + parts[0].shape[1:], BF)] * outs,
        compiler_params=params(),
        name="sum_parts",
    )(*parts)


def finish_kernel(pos_ref, *refs, factor):
    parts = refs[:4]
    mix_ref, project_ref, output_ref, gain_ref, pj, ex = refs[4:]
    my_m = pos_ref[1]
    for c in range(2):
        for rx in range(2):
            for rz in range(4):
                m = my_m ^ (rz * 4 + rx * 2 + c)
                piece = parts[c * 2 + rx][rz].astype(F32) * factor
                start = pl.multiple_of((m % 8) * 32, 32)
                for n in range(4):
                    mix_ref[m // 8, pl.ds(start, 32), n * E : (n + 1) * E] = piece[
                        n * 32 : (n + 1) * 32
                    ]
                pj[m] = piece[128:136]
                ex[m] = piece[136:144]
    for l in range(LAYERS):
        rows = [
            jnp.concatenate([pj[l * 8 + h * 4 + kb] for kb in range(4)], axis=0) for h in range(2)
        ]
        project_ref[l] = jnp.concatenate(rows, axis=1).T
        for b in range(2):
            output_ref[l, b * 8 : (b + 1) * 8, :] = ex[l * 2 + b]
        gain_ref[l : l + 1, :] = ex[4][0:1, l * 64 : (l + 1) * 64]


def finish(pos, parts, factor):
    vmem = pl.BlockSpec(memory_space=pltpu.VMEM)
    return pl.pallas_call(
        functools.partial(finish_kernel, factor=factor),
        out_shape=[
            jax.ShapeDtypeStruct((LAYERS, F // 2, F), F32),
            jax.ShapeDtypeStruct((LAYERS, F // 2, K), F32),
            jax.ShapeDtypeStruct((LAYERS, K // 2, E), F32),
            jax.ShapeDtypeStruct((LAYERS, E // 2), F32),
        ],
        in_specs=[pl.BlockSpec(memory_space=pltpu.SMEM)] + [vmem] * 4,
        out_specs=[vmem] * 4,
        scratch_shapes=[pltpu.VMEM((16, 8, E), F32)] * 2,
        compiler_params=params(),
        name="finish",
    )(pos, *parts)


def reduce_packed(pos, keep, send, factor):
    other = across(send, 0, 1)
    own, to_y, to_x, to_xy = sum_parts([keep, other], 4)
    parts = [own, across(to_y, 1, 0), across(to_x, 0, 2), across(to_xy, 1, 2)]
    quarters = sum_parts(parts, 4)
    parts = [quarters[0]] + [across(quarters[r], 0, 4 * r) for r in range(1, 4)]
    (piece,) = sum_parts(parts, 1)
    column = jnp.concatenate([piece] + [across(piece, 0, 4 * r) for r in range(1, 4)], axis=0)
    beside = across(column, 0, 2)
    return finish(pos, [column, beside, across(column, 0, 1), across(beside, 0, 1)], factor)


def per_device(
    table_rows,
    bag_ids,
    slot_feature,
    block_exponent,
    fm_project,
    fm_output,
    mix_weight,
    norm_gain,
    out_cotangent,
):
    tables, groups = lax.axis_size("mp"), lax.axis_size("dp")
    f_dev = F // tables
    bags = SAMP_DEV * tables * f_dev
    rows = table_rows.shape[2]
    ids = bag_ids.reshape(1, rows)
    factor = 1.0 / float(SAMP_DEV * tables * groups) ** 0.5
    pos = jnp.stack([lax.axis_index("dp"), lax.axis_index("mp")]).astype(jnp.int32)

    pooled = pool(ids, table_rows.reshape(rows, E), bags).reshape(tables, SAMP_DEV * f_dev, E)
    recv = lax.all_to_all(pooled, "mp", split_axis=0, concat_axis=0, tiled=True)
    project, output, mix, gain = (
        gather_dp(part, 1) for part in (fm_project, fm_output, mix_weight, norm_gain)
    )
    operands = prepare(slot_feature, block_exponent, project, output, mix)
    packed = (groups, tables) == (2, 16)
    feats, slots, *grads = run_layers(
        pos, recv, out_cotangent, operands, project, gain, f_dev, packed
    )
    owner = lax.all_to_all(slots, "mp", split_axis=0, concat_axis=0, tiled=True)
    row_grads = expand(ids, owner.reshape(bags, E), rows).reshape(1, 1, rows, E)
    if packed:
        mix_g, project_g, output_g, gain_g = reduce_packed(pos, grads[0], grads[1], factor)
        return feats, row_grads, project_g, output_g, mix_g, gain_g
    summed = lax.psum(tuple(grads), "mp")
    mix_g, project_t, output_g, gain_g = summed
    parts = (project_t.transpose(0, 2, 1), output_g, mix_g, gain_g)
    shares = [
        lax.psum_scatter(part.astype(BF), "dp", scatter_dimension=1, tiled=True).astype(F32)
        * factor
        for part in parts
    ]
    return feats, row_grads, *shares


def solution(mesh):
    placed = (
        P("dp", "mp", None, None),
        P("dp", "mp", None),
        P(),
        P(),
        P(None, "dp", None),
        P(None, "dp", None),
        P(None, "dp", None),
        P(None, "dp"),
        P(("dp", "mp"), None, None),
    )
    return jax.shard_map(
        per_device,
        mesh=mesh,
        in_specs=placed,
        out_specs=(
            P(("dp", "mp"), None, None),
            P("dp", "mp", None, None),
            P(None, "dp", None),
            P(None, "dp", None),
            P(None, "dp", None),
            P(None, "dp"),
        ),
        check_vma=False,
    )
```

```python
import functools

import jax
import jax.numpy as jnp
from jax import lax
from jax.experimental import pallas as pl
from jax.experimental.pallas import tpu as pltpu
from jax.sharding import PartitionSpec as P

F = 512
E = 128
K = 32
LAYERS = 2
SAMP_DEV = 8
PAIR = 2
PW = PAIR * E
PAIRS = SAMP_DEV // PAIR
CHUNK = 128
EPS = 1e-05
VMEM_LIMIT = 62 * 1024 * 1024
PIECE = 144
BF = jnp.bfloat16
F32 = jnp.float32


def params():
    return pltpu.CompilerParams(vmem_limit_bytes=VMEM_LIMIT)


def dot(left, right):
    return jnp.dot(left, right, preferred_element_type=F32)


def dot_nt(left, right):
    return lax.dot_general(left, right, (((1,), (1,)), ((), ())), preferred_element_type=F32)


def dot_tn(left, right):
    return lax.dot_general(left, right, (((0,), (0,)), ((), ())), preferred_element_type=F32)


class Copies:
    def __init__(self, sems):
        self.sems, self.used, self.open = sems, 0, {}

    def start(self, key, source, target):
        copy = pltpu.make_async_copy(source, target, self.sems.at[self.used])
        self.used += 1
        copy.start()
        self.open[key] = copy

    def wait(self, *keys):
        for key in keys:
            if key in self.open:
                self.open.pop(key).wait()

    def drain(self):
        self.wait(*list(self.open))


BLOCK = 128
ANY = pl.BlockSpec(memory_space=pltpu.HBM)
VMEM = pl.BlockSpec(memory_space=pltpu.VMEM)


def pool_kernel(ids_ref, rows_ref, out_ref):
    bags, rows = out_ref.shape[0], rows_ref.shape[0]
    for low in range(0, bags, BLOCK):
        high = min(low + BLOCK + rows - bags, rows)
        bag = lax.broadcasted_iota(jnp.int32, (BLOCK, high - low), 0) + low
        hot = jnp.where(ids_ref[:, low:high] == bag, 1.0, 0.0).astype(BF)
        out_ref[low : low + BLOCK, :] = dot(hot, rows_ref[low:high, :]).astype(BF)


def pool(ids, rows, bags):
    return pl.pallas_call(
        pool_kernel,
        out_shape=jax.ShapeDtypeStruct((bags, E), BF),
        compiler_params=params(),
        name="pool",
    )(ids, rows)


def expand_kernel(ids_ref, bags_ref, out_ref, table):
    rows, bags = out_ref.shape[0], bags_ref.shape[0]
    table[...] = jnp.zeros_like(table)
    for part in range(rows // BLOCK):
        table[part : part + 1, :] = ids_ref[:, part * BLOCK : (part + 1) * BLOCK]
    columns = table[...].T
    for part in range(rows // BLOCK):
        low = part * BLOCK
        first = max(low - (rows - bags), 0)
        last = min(low + BLOCK, bags)
        bag = lax.broadcasted_iota(jnp.int32, (BLOCK, last - first), 1) + first
        hot = jnp.where(columns[:, part : part + 1] == bag, 1.0, 0.0).astype(BF)
        out_ref[low : low + BLOCK, :] = dot(hot, bags_ref[first:last, :]).astype(BF)


def expand(ids, owner, rows):
    return pl.pallas_call(
        expand_kernel,
        out_shape=jax.ShapeDtypeStruct((rows, E), BF),
        scratch_shapes=[pltpu.VMEM((BLOCK, BLOCK), jnp.int32)],
        compiler_params=params(),
        name="expand",
    )(ids, owner)


def prepare_kernel(pos_ref, slot_ref, expo_ref, *refs, halves):
    weights, outs = refs[: 4 * halves], refs[4 * halves :]
    projects, outputs, mixes, gains = (weights[n * halves : (n + 1) * halves] for n in range(4))
    left_ref, back_ref, diag_ref, project_ref, gain_ref, scale_ref, perm_ref, unperm_ref = outs
    first = pos_ref[0] == 0

    def joined(parts, axis):
        if halves == 1:
            return parts[0]
        return jnp.where(
            first, jnp.concatenate(parts, axis=axis), jnp.concatenate(parts[::-1], axis=axis)
        )

    for layer in range(LAYERS):
        for half in range(halves):
            size = F // halves
            start = 0 if halves == 1 else pl.multiple_of((pos_ref[0] ^ half) * size, size)
            left_ref[layer, pl.ds(start, size), :] = mixes[half][layer]
        back_ref[layer] = left_ref[layer, :F, :].T
        project_t = joined([ref[layer] for ref in projects], 1)
        left_ref[layer, F:, :] = project_t
        none = jnp.zeros((PAIR * K, F), BF)
        project_ref[layer] = jnp.concatenate([none, project_t, none[:K]], axis=0).T
        row = joined([ref[layer].astype(F32) for ref in outputs], 0).astype(BF)
        none = jnp.zeros_like(row)
        diag_ref[layer] = jnp.concatenate(
            [
                jnp.concatenate([row, none], axis=1),
                jnp.concatenate([none, row], axis=1),
                jnp.zeros((E - PAIR * K, PW), BF),
            ],
            axis=0,
        )
    gain_ref[...] = joined([ref[...].astype(F32) for ref in gains], 1)
    expo = expo_ref[...]
    small = jnp.where(
        expo == 0, 0.25, jnp.where(expo == 1, 0.5, jnp.where(expo == 2, 1.0, 2.0))
    ).astype(BF)
    blocks = expo.shape[0]
    spread = jnp.where(
        lax.broadcasted_iota(jnp.int32, (blocks, E), 1) // (E // blocks)
        == lax.broadcasted_iota(jnp.int32, (blocks, E), 0),
        1.0,
        0.0,
    ).astype(BF)
    scale_ref[...] = dot_tn(small, spread)
    hot = jnp.where(slot_ref[...] == lax.broadcasted_iota(jnp.int32, (F, F), 0), 1.0, 0.0)
    perm_ref[...] = hot.astype(BF)
    unperm_ref[...] = hot.T.astype(BF)


def prepare(pos, slot_feature, block_exponent, weights):
    halves = len(weights[0])
    flat = [part for parts in weights for part in parts]
    return pl.pallas_call(
        functools.partial(prepare_kernel, halves=halves),
        out_shape=(
            jax.ShapeDtypeStruct((LAYERS, F + K, F), BF),
            jax.ShapeDtypeStruct((LAYERS, F, F), BF),
            jax.ShapeDtypeStruct((LAYERS, E, PW), BF),
            jax.ShapeDtypeStruct((LAYERS, F, E), BF),
            jax.ShapeDtypeStruct((LAYERS, E), F32),
            jax.ShapeDtypeStruct((F, E), F32),
            jax.ShapeDtypeStruct((F, F), BF),
            jax.ShapeDtypeStruct((F, F), BF),
        ),
        in_specs=[pl.BlockSpec(memory_space=pltpu.SMEM)] + [VMEM] * (2 + len(flat)),
        out_specs=(VMEM,) * 8,
        compiler_params=params(),
        name="prepare",
    )(pos, slot_feature.reshape(1, F), block_exponent.T, *flat)


def unslot(block, f_dev):
    if f_dev % 16:
        block = block.astype(F32)
    parts = [block[:, t * f_dev : (t + 1) * f_dev, :].reshape(F, E) for t in range(PAIR)]
    return jnp.concatenate(parts, axis=1).astype(BF)


CONSTANTS = ("perm", "scale", "left", "diag", "back", "project", "unperm")


def layers_kernel(pos_ref, gain_ref, recv_hbm, cot_hbm, *refs, f_dev, packed):
    sources, refs = dict(zip(CONSTANTS, refs)), refs[len(CONSTANTS) :]
    feats_hbm, slots_hbm = refs[:2]
    grads = 2 if packed else 4
    grad_outs, refs = refs[2 : 2 + grads], refs[2 + grads :]
    held, refs = dict(zip(CONSTANTS, refs)), refs[len(CONSTANTS) :]
    recv_ref, cot_ref, feats_ref, slots_ref = refs[:4]
    grad_refs, refs = refs[4 : 4 + grads], refs[4 + grads :]
    xs, ts, normed_s, inv_s, grad_s, next_s, wacc, gacc, dm, pj, ex, sems = refs
    left_ref, back_ref, diag_ref = held["left"], held["back"], held["diag"]
    project_ref, scale_ref = held["project"], held["scale"]
    copies = Copies(sems)

    def slot_rows(p):
        return slice(p * PAIR * f_dev, (p + 1) * PAIR * f_dev)

    def fetch(name):
        copies.start(name, sources[name], held[name])

    copies.start("recv", recv_hbm, recv_ref)
    for name in ("perm", "scale", "left", "diag"):
        fetch(name)
    copies.start("cot", cot_hbm, cot_ref)
    for name in ("back", "project", "unperm"):
        fetch(name)

    wacc[...] = jnp.zeros_like(wacc)
    gacc[...] = jnp.zeros_like(gacc)

    def pair_steps(p):
        columns = slice(p * PW, (p + 1) * PW)
        x = dot(held["perm"][...], unslot(recv_ref[:, slot_rows(p)], f_dev))
        scale = scale_ref[...]
        x = (x * jnp.concatenate([scale] * PAIR, axis=1)).astype(BF)
        same = (
            lax.broadcasted_iota(jnp.int32, (PAIR * K, PW), 0) // K
            == lax.broadcasted_iota(jnp.int32, (PAIR * K, PW), 1) // E
        )
        saved = []
        for layer in range(LAYERS):
            xs[layer, :, columns] = x
            mixed = dot(left_ref[layer], x)
            projected = jnp.concatenate([mixed[F:]] * PAIR, axis=0)
            projected = jnp.where(same, projected, 0.0).astype(BF)
            paired = dot_nt(x, projected).astype(BF)
            low = dot(paired, diag_ref[layer, : PAIR * K])
            gain = gain_ref[layer : layer + 1, :]
            saved.append((x, projected, paired))
            yield
            for t in range(PAIR):
                lanes = slice(t * E, (t + 1) * E)
                for r in range(0, F, CHUNK):
                    rows = slice(r, r + CHUNK)
                    total = x[rows, lanes].astype(F32) + mixed[rows, lanes] + low[rows, lanes]
                    centred = total - jnp.sum(total, axis=-1, keepdims=True) * (1.0 / E)
                    variance = jnp.sum(centred * centred, axis=-1, keepdims=True) * (1.0 / E)
                    inverse = lax.rsqrt(variance + EPS)
                    normed = centred * inverse
                    normed_s[p, layer, rows, lanes] = normed
                    inv_s[p, layer, rows, lanes] = jnp.broadcast_to(inverse, (CHUNK, E))
                    out = (normed * gain).astype(BF)
                    if layer == LAYERS - 1:
                        feats_ref[p * PAIR + t, rows, :] = out
                    else:
                        next_s[p, rows, lanes] = out
            yield
            x = next_s[p]

        for layer in reversed(range(LAYERS)):
            x, projected, paired = saved[layer]
            gain = gain_ref[layer : layer + 1, :]
            dgain = jnp.zeros((8, E), F32)
            for t in range(PAIR):
                lanes = slice(t * E, (t + 1) * E)
                for r in range(0, F, CHUNK):
                    rows = slice(r, r + CHUNK)
                    if layer == LAYERS - 1:
                        upper = cot_ref[p * PAIR + t, rows, :].astype(F32)
                    else:
                        upper = next_s[p, rows, lanes].astype(F32)
                    normed = normed_s[p, layer, rows, lanes]
                    dgain = dgain + jnp.sum((upper * normed).reshape(CHUNK // 8, 8, E), axis=0)
                    scaled = upper * gain
                    first = jnp.sum(scaled, axis=-1, keepdims=True) * (1.0 / E)
                    second = jnp.sum(scaled * normed, axis=-1, keepdims=True) * (1.0 / E)
                    total = inv_s[p, layer, rows, lanes] * (scaled - first - normed * second)
                    grad_s[p, rows, lanes] = total
                    next_s[p, rows, lanes] = total.astype(BF)
            gacc[layer] += dgain
            yield
            total_low = next_s[p]
            ts[layer, :F, columns] = total_low
            grad_paired = dot_nt(total_low, diag_ref[layer]).astype(BF)
            wide = dot_tn(grad_paired[:, : PAIR * K], x)
            grad_projected = jnp.concatenate(
                [wide[t * K : (t + 1) * K, t * E : (t + 1) * E] for t in range(PAIR)], axis=1
            ).astype(BF)
            ts[layer, F:, columns] = grad_projected
            wide = dot_tn(paired, total_low)
            for t in range(PAIR):
                wacc[layer] += wide[t * K : (t + 1) * K, t * E : (t + 1) * E]
            rest = jnp.zeros((E - (PAIR + 1) * K, PW), BF)
            upstream = dot(back_ref[layer], total_low) + dot(
                grad_paired + project_ref[layer],
                jnp.concatenate([projected, grad_projected, rest], axis=0),
            )
            yield
            for t in range(PAIR):
                lanes = slice(t * E, (t + 1) * E)
                for r in range(0, F, CHUNK):
                    rows = slice(r, r + CHUNK)
                    out = (grad_s[p, rows, lanes] + upstream[rows, lanes]).astype(BF)
                    if layer == 0:
                        out = (out.astype(F32) * scale_ref[rows]).astype(BF)
                    next_s[p, rows, lanes] = out

        slots = dot(held["unperm"][...], next_s[p])
        if f_dev % 16 == 0:
            slots = slots.astype(BF)
        for t in range(PAIR):
            low = (p * PAIR + t) * f_dev
            slots_ref[:, low : low + f_dev, :] = (
                slots[:, t * E : (t + 1) * E].reshape(F // f_dev, f_dev, E).astype(BF)
            )
        yield

    def weight_grads(layer):
        dm[layer] = dot_nt(ts[layer], xs[layer])
        gain_row = jnp.sum(gacc[layer], axis=0, keepdims=True)
        if not packed:
            mix_ref, project_t_ref, output_ref, gain_out_ref = grad_refs
            mix_ref[layer] = dm[layer, :F, :]
            project_t_ref[layer] = dm[layer, F:, :]
            output_ref[layer] = wacc[layer]
            gain_out_ref[layer : layer + 1, :] = gain_row
            return
        half = F // 2
        for d in range(2):
            for q in range(8):
                low = d * half + (q // 4) * E
                pj[d, layer * 8 + q] = dm[
                    layer, F + 8 * (q % 4) : F + 8 * (q % 4) + 8, low : low + E
                ]
                if q < 2:
                    low = d * (K // 2) + 8 * q
                    ex[d, layer * 8 + q] = wacc[layer, low : low + 8, :]
                else:
                    row = gain_row[:, d * 64 : (d + 1) * 64]
                    ex[d, layer * 8 + q] = jnp.broadcast_to(
                        jnp.concatenate([row, row], axis=1), (8, E)
                    )
        my_d, my_m = pos_ref[0], pos_ref[1]
        flip = (my_m >> 3) ^ layer
        for core in range(2):
            for rx in range(2):
                for ry in range(2):
                    for low_z in range(2):
                        q = (my_m & 7) ^ (low_z * 4 + rx * 2 + core)
                        d = my_d ^ ry
                        start = pl.multiple_of(d * half + q * 32, 32)
                        block = dm[layer, pl.ds(start, 32), :]
                        pieces = [block[:, c * E : (c + 1) * E] for c in range(4)]
                        pieces += [pj[d, layer * 8 + q], ex[d, layer * 8 + q]]
                        place = (rx * 2 + ry) * 4 + low_z + 2 * flip
                        grad_refs[core][place] = jnp.concatenate(pieces, axis=0).astype(BF)

    programs = [pair_steps(p) for p in range(PAIRS)]
    phases = 4 * LAYERS + 1
    for tick in range(phases + PAIRS - 1):
        if tick == 0:
            copies.wait("recv", "perm", "scale", "left", "diag")
        if tick == 2 * LAYERS:
            copies.wait("cot", "back", "project", "unperm")
        if tick == 2 * LAYERS + PAIRS - 1:
            copies.start("feats", feats_ref, feats_hbm)
        for p in range(PAIRS):
            if 0 <= tick - p < phases:
                next(programs[p])
        for layer in reversed(range(LAYERS)):
            if tick - (PAIRS - 1) == phases - 2 - 2 * layer:
                weight_grads(layer)
    copies.start("slots", slots_ref, slots_hbm)
    for n in range(grads):
        copies.start(("grad", n), grad_refs[n], grad_outs[n])
    copies.drain()


def run_layers(pos, recv, cotangent, operands, f_dev, packed):
    left, back, diag, project, gain, scale, perm, unperm = operands
    tables = F // f_dev

    def shape(dims, dtype=F32):
        return jax.ShapeDtypeStruct(dims, dtype)

    if packed:
        grads = [shape((16, PIECE, E), BF)] * 2
    else:
        grads = [
            shape((LAYERS, F, F)),
            shape((LAYERS, K, F)),
            shape((LAYERS, K, E)),
            shape((LAYERS, E)),
        ]
    given = dict(
        perm=perm, scale=scale, left=left, diag=diag, back=back, project=project, unperm=unperm
    )
    constants = [given[name] for name in CONSTANTS]
    width = SAMP_DEV * E
    big = [shape((SAMP_DEV, F, E), BF), shape((tables, SAMP_DEV * f_dev, E), BF)]
    outs = big + grads

    def scratch(x):
        return pltpu.VMEM(x.shape, x.dtype)

    copies = len(constants) + 4 + len(grads)
    return pl.pallas_call(
        functools.partial(layers_kernel, f_dev=f_dev, packed=packed),
        out_shape=outs,
        in_specs=[pl.BlockSpec(memory_space=pltpu.SMEM), VMEM] + [ANY] * (2 + len(constants)),
        out_specs=[ANY] * len(outs),
        scratch_shapes=[scratch(x) for x in constants]
        + [scratch(recv), scratch(cotangent)]
        + [scratch(x) for x in outs]
        + [
            pltpu.VMEM((LAYERS, F, width), BF),
            pltpu.VMEM((LAYERS, F + K, width), BF),
            pltpu.VMEM((PAIRS, LAYERS, F, PW), F32),
            pltpu.VMEM((PAIRS, LAYERS, F, PW), F32),
            pltpu.VMEM((PAIRS, F, PW), F32),
            pltpu.VMEM((PAIRS, F, PW), BF),
            pltpu.VMEM((LAYERS, K, E), F32),
            pltpu.VMEM((LAYERS, 8, E), F32),
            pltpu.VMEM((LAYERS, F + K, F), F32),
            pltpu.VMEM((2, 16, 8, E), F32),
            pltpu.VMEM((2, 16, 8, E), F32),
            pltpu.SemaphoreType.DMA((copies,)),
        ],
        compiler_params=params(),
        name="layers",
    )(pos, gain, recv, cotangent, *constants)


def across(x, d, m):
    pairs = [(i, i ^ (d * 16 + m)) for i in range(32)]
    return lax.ppermute(x, ("dp", "mp"), pairs)


def added(parts):
    return sum(part.astype(F32) for part in parts).astype(BF)


def finish_kernel(pos_ref, *refs, factor):
    parts = refs[:4]
    mix_ref, project_ref, output_ref, gain_ref, pj, ex = refs[4:]
    my_m = pos_ref[1]
    for c in range(2):
        for rx in range(2):
            for rz in range(4):
                m = my_m ^ (rz * 4 + rx * 2 + c)
                piece = parts[c * 2 + rx][rz].astype(F32) * factor
                start = pl.multiple_of((m & 7) * 32, 32)
                for n in range(4):
                    mix_ref[m >> 3, pl.ds(start, 32), n * E : (n + 1) * E] = piece[
                        n * 32 : (n + 1) * 32
                    ]
                pj[m] = piece[128:136]
                ex[m] = piece[136:144]
    for l in range(LAYERS):
        for h in range(2):
            for b in range(4):
                project_ref[l, b * 8 : (b + 1) * 8, h * E : (h + 1) * E] = pj[l * 8 + h * 4 + b]
        for b in range(2):
            output_ref[l, b * 8 : (b + 1) * 8, :] = ex[l * 8 + b]
        gain_ref[l : l + 1, :] = ex[l * 8 + 2][0:1, :64]


def finish(pos, parts, factor):
    return pl.pallas_call(
        functools.partial(finish_kernel, factor=factor),
        out_shape=[
            jax.ShapeDtypeStruct((LAYERS, F // 2, F), F32),
            jax.ShapeDtypeStruct((LAYERS, K, F // 2), F32),
            jax.ShapeDtypeStruct((LAYERS, K // 2, E), F32),
            jax.ShapeDtypeStruct((LAYERS, E // 2), F32),
        ],
        in_specs=[pl.BlockSpec(memory_space=pltpu.SMEM)] + [VMEM] * 4,
        out_specs=[VMEM] * 4,
        scratch_shapes=[pltpu.VMEM((16, 8, E), F32)] * 2,
        compiler_params=params(),
        name="finish",
    )(pos, *parts)


def exchange(x):
    return lax.all_to_all(x, "mp", split_axis=0, concat_axis=0, tiled=True)


def return_packed(pos, slots, keep, send, ids, factor):
    rows, bags = ids.shape[1], slots.shape[0] * slots.shape[1]
    other = across(send, 0, 1)
    own, to_y, to_x, to_xy = [
        added([part[4 * r : 4 * r + 4] for part in (keep, other)]) for r in range(4)
    ]
    parts = [own, across(to_y, 1, 0), across(to_x, 0, 2), across(to_xy, 1, 2)]
    owner = exchange(slots)
    quarters = [added([part[r : r + 1] for part in parts]) for r in range(4)]
    parts = [quarters[0]] + [across(quarters[r], 0, 4 * r) for r in range(1, 4)]
    piece = added(parts)
    column = jnp.concatenate([piece] + [across(piece, 0, 4 * r) for r in range(1, 4)], axis=0)
    column, owner = lax.optimization_barrier((column, owner))
    beside = across(column, 0, 2)
    row_grads = expand(ids, owner.reshape(bags, E), rows)
    parts = [column, beside, across(column, 0, 1), across(beside, 0, 1)]
    parts, row_grads = lax.optimization_barrier((parts, row_grads))
    return row_grads, finish(pos, parts, factor)


def per_device(
    table_rows,
    bag_ids,
    slot_feature,
    block_exponent,
    fm_project,
    fm_output,
    mix_weight,
    norm_gain,
    out_cotangent,
):
    tables, groups = lax.axis_size("mp"), lax.axis_size("dp")
    f_dev = F // tables
    bags = SAMP_DEV * tables * f_dev
    rows = table_rows.shape[2]
    ids = bag_ids.reshape(1, rows)
    factor = 1.0 / float(SAMP_DEV * tables * groups) ** 0.5
    pos = jnp.stack([lax.axis_index("dp"), lax.axis_index("mp")]).astype(jnp.int32)

    pooled = pool(ids, table_rows.reshape(rows, E), bags).reshape(tables, SAMP_DEV * f_dev, E)
    recv = exchange(pooled)
    weights = (fm_project.transpose(0, 2, 1), fm_output, mix_weight, norm_gain)
    if groups == 2:
        weights = [(part, lax.ppermute(part, "dp", [(0, 1), (1, 0)])) for part in weights]
    else:
        weights = [
            (lax.all_gather(part, "dp", axis=axis, tiled=True),)
            for part, axis in zip(weights, (2, 1, 1, 1))
        ]
    operands = prepare(pos, slot_feature, block_exponent, weights)
    packed = (groups, tables) == (2, 16)
    feats, slots, *grads = run_layers(pos, recv, out_cotangent, operands, f_dev, packed)
    if packed:
        row_grads, shares = return_packed(pos, slots, *grads, ids, factor)
        project_t, output_g, mix_g, gain_g = shares[1], shares[2], shares[0], shares[3]
    else:
        row_grads = expand(ids, exchange(slots).reshape(bags, E), rows)
        mix_g, project_t, output_g, gain_g = (
            lax.psum_scatter(part.astype(BF), "dp", scatter_dimension=axis, tiled=True).astype(F32)
            * factor
            for part, axis in zip(lax.psum(tuple(grads), "mp"), (1, 2, 1, 1))
        )
    return (
        feats,
        row_grads.reshape(1, 1, rows, E),
        project_t.transpose(0, 2, 1),
        output_g,
        mix_g,
        gain_g,
    )


def solution(mesh):
    placed = (
        P("dp", "mp", None, None),
        P("dp", "mp", None),
        P(),
        P(),
        P(None, "dp", None),
        P(None, "dp", None),
        P(None, "dp", None),
        P(None, "dp"),
        P(("dp", "mp"), None, None),
    )
    return jax.shard_map(
        per_device,
        mesh=mesh,
        in_specs=placed,
        out_specs=(
            P(("dp", "mp"), None, None),
            P("dp", "mp", None, None),
            P(None, "dp", None),
            P(None, "dp", None),
            P(None, "dp", None),
            P(None, "dp"),
        ),
        check_vma=False,
    )
```

```python
import functools

import jax
import jax.numpy as jnp
from jax import lax
from jax.experimental import pallas as pl
from jax.experimental.pallas import tpu as pltpu
from jax.sharding import PartitionSpec as P

F = 512
E = 128
K = 32
LAYERS = 2
SAMP_DEV = 8
PAIR = 4
PW = PAIR * E
PAIRS = SAMP_DEV // PAIR
CHUNK = 128
EPS = 1e-05
MIB = 1024 * 1024
WHOLE, PART = 62, 46
PIECE = 144
BF = jnp.bfloat16
F32 = jnp.float32


def params(mib):
    return pltpu.CompilerParams(vmem_limit_bytes=mib * MIB)


def dot(left, right):
    return jnp.dot(left, right, preferred_element_type=F32)


def dot_nt(left, right):
    return lax.dot_general(left, right, (((1,), (1,)), ((), ())), preferred_element_type=F32)


def dot_tn(left, right):
    return lax.dot_general(left, right, (((0,), (0,)), ((), ())), preferred_element_type=F32)


class Copies:
    def __init__(self, sems):
        self.sems, self.used, self.open = sems, 0, {}

    def start(self, key, source, target):
        copy = pltpu.make_async_copy(source, target, self.sems.at[self.used])
        self.used += 1
        copy.start()
        self.open[key] = copy

    def wait(self, *keys):
        for key in keys:
            if key in self.open:
                self.open.pop(key).wait()

    def drain(self):
        self.wait(*list(self.open))


BLOCK = 128
HBM = pl.BlockSpec(memory_space=pltpu.HBM)
VMEM = pl.BlockSpec(memory_space=pltpu.VMEM)


def pool_kernel(ids_ref, rows_ref, out_ref):
    bags, rows = out_ref.shape[0], rows_ref.shape[0]
    for low in range(0, bags, BLOCK):
        high = min(low + BLOCK + rows - bags, rows)
        bag = lax.broadcasted_iota(jnp.int32, (BLOCK, high - low), 0) + low
        hot = jnp.where(ids_ref[:, low:high] == bag, 1.0, 0.0).astype(BF)
        out_ref[low : low + BLOCK, :] = dot(hot, rows_ref[low:high, :]).astype(BF)


def pool(ids, rows, bags):
    return pl.pallas_call(
        pool_kernel,
        out_shape=jax.ShapeDtypeStruct((bags, E), BF),
        compiler_params=params(WHOLE),
        name="pool",
    )(ids, rows)


def expand_kernel(ids_ref, bags_ref, out_ref, table):
    rows, bags = out_ref.shape[0], bags_ref.shape[0]
    table[...] = jnp.zeros_like(table)
    for part in range(rows // BLOCK):
        table[part : part + 1, :] = ids_ref[:, part * BLOCK : (part + 1) * BLOCK]
    columns = table[...].T
    for part in range(rows // BLOCK):
        low = part * BLOCK
        first = max(low - (rows - bags), 0)
        last = min(low + BLOCK, bags)
        bag = lax.broadcasted_iota(jnp.int32, (BLOCK, last - first), 1) + first
        hot = jnp.where(columns[:, part : part + 1] == bag, 1.0, 0.0).astype(BF)
        out_ref[low : low + BLOCK, :] = dot(hot, bags_ref[first:last, :]).astype(BF)


def expand(ids, owner, rows):
    return pl.pallas_call(
        expand_kernel,
        out_shape=jax.ShapeDtypeStruct((rows, E), BF),
        scratch_shapes=[pltpu.VMEM((BLOCK, BLOCK), jnp.int32)],
        compiler_params=params(PART),
        name="expand",
    )(ids, owner)


def prepare_kernel(pos_ref, slot_ref, expo_ref, *refs, halves):
    weights, outs = refs[: 4 * halves], refs[4 * halves :]
    projects, outputs, mixes, gains = (weights[n * halves : (n + 1) * halves] for n in range(4))
    left_ref, back_ref, diag_ref, project_ref, gain_ref, scale_ref, perm_ref, unperm_ref = outs
    first = pos_ref[0] == 0

    def joined(parts, axis):
        if halves == 1:
            return parts[0]
        return jnp.where(
            first, jnp.concatenate(parts, axis=axis), jnp.concatenate(parts[::-1], axis=axis)
        )

    for layer in range(LAYERS):
        for half in range(halves):
            size = F // halves
            start = 0 if halves == 1 else pl.multiple_of((pos_ref[0] ^ half) * size, size)
            left_ref[layer, pl.ds(start, size), :] = mixes[half][layer]
        back_ref[layer] = left_ref[layer, :F, :].T
        project_t = joined([ref[layer] for ref in projects], 1)
        left_ref[layer, F:, :] = project_t
        none = jnp.zeros((E - K, F), BF)
        project_ref[layer] = jnp.concatenate([project_t, none], axis=0).T
        row = joined([ref[layer].astype(F32) for ref in outputs], 0).astype(BF)
        diag_ref[layer] = jnp.zeros((PAIR * K, PW), BF)
        for t in range(PAIR):
            diag_ref[layer, t * K : (t + 1) * K, t * E : (t + 1) * E] = row
    gain_ref[...] = joined([ref[...].astype(F32) for ref in gains], 1)
    expo = expo_ref[...]
    small = jnp.where(
        expo == 0, 0.25, jnp.where(expo == 1, 0.5, jnp.where(expo == 2, 1.0, 2.0))
    ).astype(BF)
    blocks = expo.shape[0]
    spread = jnp.where(
        lax.broadcasted_iota(jnp.int32, (blocks, E), 1) // (E // blocks)
        == lax.broadcasted_iota(jnp.int32, (blocks, E), 0),
        1.0,
        0.0,
    ).astype(BF)
    scale_ref[...] = dot_tn(small, spread)
    hot = jnp.where(slot_ref[...] == lax.broadcasted_iota(jnp.int32, (F, F), 0), 1.0, 0.0)
    perm_ref[...] = hot.astype(BF)
    unperm_ref[...] = hot.T.astype(BF)


def prepare(pos, slot_feature, block_exponent, weights):
    halves = len(weights[0])
    flat = [part for parts in weights for part in parts]
    return pl.pallas_call(
        functools.partial(prepare_kernel, halves=halves),
        out_shape=(
            jax.ShapeDtypeStruct((LAYERS, F + K, F), BF),
            jax.ShapeDtypeStruct((LAYERS, F, F), BF),
            jax.ShapeDtypeStruct((LAYERS, PAIR * K, PW), BF),
            jax.ShapeDtypeStruct((LAYERS, F, E), BF),
            jax.ShapeDtypeStruct((LAYERS, E), F32),
            jax.ShapeDtypeStruct((F, E), F32),
            jax.ShapeDtypeStruct((F, F), BF),
            jax.ShapeDtypeStruct((F, F), BF),
        ),
        in_specs=[pl.BlockSpec(memory_space=pltpu.SMEM)] + [VMEM] * (2 + len(flat)),
        out_specs=(VMEM,) * 8,
        compiler_params=params(WHOLE),
        name="prepare",
    )(pos, slot_feature.reshape(1, F), block_exponent.T, *flat)


def unslot(block, f_dev):
    if f_dev % 16:
        block = block.astype(F32)
    parts = [block[:, t * f_dev : (t + 1) * f_dev, :].reshape(F, E) for t in range(PAIR)]
    return jnp.concatenate(parts, axis=1).astype(BF)


CONSTANTS = ("perm", "scale", "left", "diag", "back", "project", "unperm")


def layers_kernel(pos_ref, gain_ref, recv_ref, cot_hbm, *refs, f_dev, packed):
    sources, refs = dict(zip(CONSTANTS, refs)), refs[len(CONSTANTS) :]
    feats_hbm, slots_hbm = refs[:2]
    grads = 2 if packed else 4
    grad_outs, refs = refs[2 : 2 + grads], refs[2 + grads :]
    held, refs = dict(zip(CONSTANTS, refs)), refs[len(CONSTANTS) :]
    cot_ref, feats_ref, slots_ref = refs[:3]
    grad_refs, refs = refs[3 : 3 + grads], refs[3 + grads :]
    xs, ts, normed_s, inv_s, grad_s, next_s, wacc, gacc, dm, pj, ex, sems = refs
    left_ref, back_ref, diag_ref = held["left"], held["back"], held["diag"]
    project_ref, scale_ref = held["project"], held["scale"]
    copies = Copies(sems)

    def slot_rows(p):
        return slice(p * PAIR * f_dev, (p + 1) * PAIR * f_dev)

    def fetch(name):
        copies.start(name, sources[name], held[name])

    for name in ("perm", "scale", "left", "diag"):
        fetch(name)
    copies.start("cot", cot_hbm, cot_ref)
    for name in ("back", "project", "unperm"):
        fetch(name)

    wacc[...] = jnp.zeros_like(wacc)
    gacc[...] = jnp.zeros_like(gacc)

    def pair_steps(p):
        columns = slice(p * PW, (p + 1) * PW)
        x = dot(held["perm"][...], unslot(recv_ref[:, slot_rows(p)], f_dev))
        scale = scale_ref[...]
        x = (x * jnp.concatenate([scale] * PAIR, axis=1)).astype(BF)
        yield
        same = (
            lax.broadcasted_iota(jnp.int32, (PAIR * K, PW), 0) // K
            == lax.broadcasted_iota(jnp.int32, (PAIR * K, PW), 1) // E
        )
        saved = []
        for layer in range(LAYERS):
            xs[layer, :, columns] = x
            mixed = dot(left_ref[layer], x)
            projected = jnp.concatenate([mixed[F:]] * PAIR, axis=0)
            projected = jnp.where(same, projected, 0.0).astype(BF)
            paired = dot_nt(x, projected).astype(BF)
            low = dot(paired, diag_ref[layer])
            gain = gain_ref[layer : layer + 1, :]
            saved.append((x, projected, paired))
            yield
            for t in range(PAIR):
                lanes = slice(t * E, (t + 1) * E)
                for r in range(0, F, CHUNK):
                    rows = slice(r, r + CHUNK)
                    total = x[rows, lanes].astype(F32) + mixed[rows, lanes] + low[rows, lanes]
                    centred = total - jnp.sum(total, axis=-1, keepdims=True) * (1.0 / E)
                    variance = jnp.sum(centred * centred, axis=-1, keepdims=True) * (1.0 / E)
                    inverse = lax.rsqrt(variance + EPS)
                    normed = centred * inverse
                    normed_s[p, layer, rows, lanes] = normed
                    inv_s[p, layer, rows, lanes] = jnp.broadcast_to(inverse, (CHUNK, E))
                    out = (normed * gain).astype(BF)
                    if layer == LAYERS - 1:
                        feats_ref[p * PAIR + t, rows, :] = out
                    else:
                        next_s[p, rows, lanes] = out
            yield
            x = next_s[p]

        for layer in reversed(range(LAYERS)):
            x, projected, paired = saved[layer]
            gain = gain_ref[layer : layer + 1, :]
            dgain = jnp.zeros((8, E), F32)
            for t in range(PAIR):
                lanes = slice(t * E, (t + 1) * E)
                for r in range(0, F, CHUNK):
                    rows = slice(r, r + CHUNK)
                    if layer == LAYERS - 1:
                        upper = cot_ref[p * PAIR + t, rows, :].astype(F32)
                    else:
                        upper = next_s[p, rows, lanes].astype(F32)
                    normed = normed_s[p, layer, rows, lanes]
                    dgain = dgain + jnp.sum((upper * normed).reshape(CHUNK // 8, 8, E), axis=0)
                    scaled = upper * gain
                    first = jnp.sum(scaled, axis=-1, keepdims=True) * (1.0 / E)
                    second = jnp.sum(scaled * normed, axis=-1, keepdims=True) * (1.0 / E)
                    total = inv_s[p, layer, rows, lanes] * (scaled - first - normed * second)
                    grad_s[p, rows, lanes] = total
                    next_s[p, rows, lanes] = total.astype(BF)
            gacc[layer] += dgain
            yield
            total_low = next_s[p]
            ts[layer, :F, columns] = total_low
            grad_paired = dot_nt(total_low, diag_ref[layer]).astype(BF)
            wide = dot_tn(grad_paired, x)
            grad_projected = jnp.concatenate(
                [wide[t * K : (t + 1) * K, t * E : (t + 1) * E] for t in range(PAIR)], axis=1
            ).astype(BF)
            ts[layer, F:, columns] = grad_projected
            wide = dot_tn(paired, total_low)
            for t in range(PAIR):
                wacc[layer] += wide[t * K : (t + 1) * K, t * E : (t + 1) * E]
            rest = jnp.zeros((E - K, PW), BF)
            upstream = dot(back_ref[layer], total_low) + dot(
                jnp.concatenate([grad_paired, project_ref[layer]], axis=1),
                jnp.concatenate([projected, grad_projected, rest], axis=0),
            )
            yield
            for t in range(PAIR):
                lanes = slice(t * E, (t + 1) * E)
                for r in range(0, F, CHUNK):
                    rows = slice(r, r + CHUNK)
                    out = (grad_s[p, rows, lanes] + upstream[rows, lanes]).astype(BF)
                    if layer == 0:
                        out = (out.astype(F32) * scale_ref[rows]).astype(BF)
                    next_s[p, rows, lanes] = out

        slots = dot(held["unperm"][...], next_s[p])
        if f_dev % 16 == 0:
            slots = slots.astype(BF)
        for t in range(PAIR):
            low = (p * PAIR + t) * f_dev
            slots_ref[:, low : low + f_dev, :] = (
                slots[:, t * E : (t + 1) * E].reshape(F // f_dev, f_dev, E).astype(BF)
            )
        yield

    def weight_grads(layer):
        dm[layer] = dot_nt(ts[layer], xs[layer])
        gain_row = jnp.sum(gacc[layer], axis=0, keepdims=True)
        if not packed:
            mix_ref, project_t_ref, output_ref, gain_out_ref = grad_refs
            mix_ref[layer] = dm[layer, :F, :]
            project_t_ref[layer] = dm[layer, F:, :]
            output_ref[layer] = wacc[layer]
            gain_out_ref[layer : layer + 1, :] = gain_row
            return
        half = F // 2
        for d in range(2):
            for q in range(8):
                low = d * half + (q // 4) * E
                pj[d, layer * 8 + q] = dm[
                    layer, F + 8 * (q % 4) : F + 8 * (q % 4) + 8, low : low + E
                ]
                if q < 2:
                    low = d * (K // 2) + 8 * q
                    ex[d, layer * 8 + q] = wacc[layer, low : low + 8, :]
                else:
                    row = gain_row[:, d * 64 : (d + 1) * 64]
                    ex[d, layer * 8 + q] = jnp.broadcast_to(
                        jnp.concatenate([row, row], axis=1), (8, E)
                    )
        my_d, my_m = pos_ref[0], pos_ref[1]
        flip = (my_m >> 3) ^ layer
        for core in range(2):
            for rx in range(2):
                for ry in range(2):
                    for low_z in range(2):
                        q = (my_m & 7) ^ (low_z * 4 + rx * 2 + core)
                        d = my_d ^ ry
                        start = pl.multiple_of(d * half + q * 32, 32)
                        block = dm[layer, pl.ds(start, 32), :]
                        pieces = [block[:, c * E : (c + 1) * E] for c in range(4)]
                        pieces += [pj[d, layer * 8 + q], ex[d, layer * 8 + q]]
                        place = (rx * 2 + ry) * 4 + low_z + 2 * flip
                        grad_refs[core][place] = jnp.concatenate(pieces, axis=0).astype(BF)

    programs = [pair_steps(p) for p in range(PAIRS)]
    phases = 4 * LAYERS + 2
    for tick in range(phases):
        if tick == 0:
            copies.wait("perm", "scale")
        if tick == 1:
            copies.wait("left", "diag")
        if tick == 2 * LAYERS + 1:
            copies.wait("cot", "back", "project", "unperm")
        if tick == 2 * LAYERS + 1:
            copies.start("feats", feats_ref, feats_hbm)
        for program in programs:
            next(program)
        for layer in reversed(range(LAYERS)):
            if tick == phases - 1 - 2 * layer:
                weight_grads(layer)
    copies.start("slots", slots_ref, slots_hbm)
    for n in range(grads):
        copies.start(("grad", n), grad_refs[n], grad_outs[n])
    copies.drain()


def run_layers(pos, recv, cotangent, operands, f_dev, packed):
    left, back, diag, project, gain, scale, perm, unperm = operands
    tables = F // f_dev

    def shape(dims, dtype=F32):
        return jax.ShapeDtypeStruct(dims, dtype)

    if packed:
        grads = [shape((16, PIECE, E), BF)] * 2
    else:
        grads = [
            shape((LAYERS, F, F)),
            shape((LAYERS, K, F)),
            shape((LAYERS, K, E)),
            shape((LAYERS, E)),
        ]
    given = dict(
        perm=perm, scale=scale, left=left, diag=diag, back=back, project=project, unperm=unperm
    )
    constants = [given[name] for name in CONSTANTS]
    width = SAMP_DEV * E
    big = [shape((SAMP_DEV, F, E), BF), shape((tables, SAMP_DEV * f_dev, E), BF)]
    outs = big + grads

    def scratch(x):
        return pltpu.VMEM(x.shape, x.dtype)

    copies = len(constants) + 3 + len(grads)
    return pl.pallas_call(
        functools.partial(layers_kernel, f_dev=f_dev, packed=packed),
        out_shape=outs,
        in_specs=[pl.BlockSpec(memory_space=pltpu.SMEM), VMEM, VMEM]
        + [HBM] * (1 + len(constants)),
        out_specs=[HBM] * len(outs),
        scratch_shapes=[scratch(x) for x in constants]
        + [scratch(cotangent)]
        + [scratch(x) for x in outs]
        + [
            pltpu.VMEM((LAYERS, F, width), BF),
            pltpu.VMEM((LAYERS, F + K, width), BF),
            pltpu.VMEM((PAIRS, LAYERS, F, PW), F32),
            pltpu.VMEM((PAIRS, LAYERS, F, PW), F32),
            pltpu.VMEM((PAIRS, F, PW), F32),
            pltpu.VMEM((PAIRS, F, PW), BF),
            pltpu.VMEM((LAYERS, K, E), F32),
            pltpu.VMEM((LAYERS, 8, E), F32),
            pltpu.VMEM((LAYERS, F + K, F), F32),
            pltpu.VMEM((2, 16, 8, E), F32),
            pltpu.VMEM((2, 16, 8, E), F32),
            pltpu.SemaphoreType.DMA((copies,)),
        ],
        compiler_params=params(58),
        name="layers",
    )(pos, gain, recv, cotangent, *constants)


def across(x, d, m):
    pairs = [(i, i ^ (d * 16 + m)) for i in range(32)]
    return lax.ppermute(x, ("dp", "mp"), pairs)


def added(parts):
    return sum(part.astype(F32) for part in parts).astype(BF)


def finish_kernel(pos_ref, *refs, factor):
    parts = refs[:4]
    mix_ref, project_ref, output_ref, gain_ref, pj, ex = refs[4:]
    my_m = pos_ref[1]
    for c in range(2):
        for rx in range(2):
            for rz in range(4):
                m = my_m ^ (rz * 4 + rx * 2 + c)
                piece = parts[c * 2 + rx][rz].astype(F32) * factor
                start = pl.multiple_of((m & 7) * 32, 32)
                for n in range(4):
                    mix_ref[m >> 3, pl.ds(start, 32), n * E : (n + 1) * E] = piece[
                        n * 32 : (n + 1) * 32
                    ]
                pj[m] = piece[128:136]
                ex[m] = piece[136:144]
    for l in range(LAYERS):
        for h in range(2):
            for b in range(4):
                project_ref[l, b * 8 : (b + 1) * 8, h * E : (h + 1) * E] = pj[l * 8 + h * 4 + b]
        for b in range(2):
            output_ref[l, b * 8 : (b + 1) * 8, :] = ex[l * 8 + b]
        gain_ref[l : l + 1, :] = ex[l * 8 + 2][0:1, :64]


def finish(pos, parts, factor):
    return pl.pallas_call(
        functools.partial(finish_kernel, factor=factor),
        out_shape=[
            jax.ShapeDtypeStruct((LAYERS, F // 2, F), F32),
            jax.ShapeDtypeStruct((LAYERS, K, F // 2), F32),
            jax.ShapeDtypeStruct((LAYERS, K // 2, E), F32),
            jax.ShapeDtypeStruct((LAYERS, E // 2), F32),
        ],
        in_specs=[pl.BlockSpec(memory_space=pltpu.SMEM)] + [VMEM] * 4,
        out_specs=[VMEM] * 4,
        scratch_shapes=[pltpu.VMEM((16, 8, E), F32)] * 2,
        compiler_params=params(PART),
        name="finish",
    )(pos, *parts)


def exchange(x):
    return lax.all_to_all(x, "mp", split_axis=0, concat_axis=0, tiled=True)


def return_packed(pos, slots, keep, send, ids, factor):
    rows, bags = ids.shape[1], slots.shape[0] * slots.shape[1]
    other = across(send, 0, 1)
    own, to_y, to_x, to_xy = [
        added([part[4 * r : 4 * r + 4] for part in (keep, other)]) for r in range(4)
    ]
    parts = [own, across(to_y, 1, 0), across(to_x, 0, 2), across(to_xy, 1, 2)]
    owner = exchange(slots)
    quarters = [added([part[r : r + 1] for part in parts]) for r in range(4)]
    parts = [quarters[0]] + [across(quarters[r], 0, 4 * r) for r in range(1, 4)]
    piece = added(parts)
    column = jnp.concatenate([piece] + [across(piece, 0, 4 * r) for r in range(1, 4)], axis=0)
    column, owner = lax.optimization_barrier((column, owner))
    beside = across(column, 0, 2)
    row_grads = expand(ids, owner.reshape(bags, E), rows)
    beside, row_grads = lax.optimization_barrier((beside, row_grads))
    parts = [column, beside, across(column, 0, 1), across(beside, 0, 1)]
    parts, row_grads = lax.optimization_barrier((parts, row_grads))
    return row_grads, finish(pos, parts, factor)


def per_device(
    table_rows,
    bag_ids,
    slot_feature,
    block_exponent,
    fm_project,
    fm_output,
    mix_weight,
    norm_gain,
    out_cotangent,
):
    tables, groups = lax.axis_size("mp"), lax.axis_size("dp")
    f_dev = F // tables
    bags = SAMP_DEV * tables * f_dev
    rows = table_rows.shape[2]
    ids = bag_ids.reshape(1, rows)
    factor = 1.0 / float(SAMP_DEV * tables * groups) ** 0.5
    pos = jnp.stack([lax.axis_index("dp"), lax.axis_index("mp")]).astype(jnp.int32)

    pooled = pool(ids, table_rows.reshape(rows, E), bags).reshape(tables, SAMP_DEV * f_dev, E)
    recv = exchange(pooled)
    weights = (fm_project.transpose(0, 2, 1), fm_output, mix_weight, norm_gain)
    if groups == 2:
        weights = [(part, lax.ppermute(part, "dp", [(0, 1), (1, 0)])) for part in weights]
    else:
        weights = [
            (lax.all_gather(part, "dp", axis=axis, tiled=True),)
            for part, axis in zip(weights, (2, 1, 1, 1))
        ]
    operands = prepare(pos, slot_feature, block_exponent, weights)
    packed = (groups, tables) == (2, 16)
    feats, slots, *grads = run_layers(pos, recv, out_cotangent, operands, f_dev, packed)
    if packed:
        row_grads, shares = return_packed(pos, slots, *grads, ids, factor)
        project_t, output_g, mix_g, gain_g = shares[1], shares[2], shares[0], shares[3]
    else:
        row_grads = expand(ids, exchange(slots).reshape(bags, E), rows)
        mix_g, project_t, output_g, gain_g = (
            lax.psum_scatter(part.astype(BF), "dp", scatter_dimension=axis, tiled=True).astype(F32)
            * factor
            for part, axis in zip(lax.psum(tuple(grads), "mp"), (1, 2, 1, 1))
        )
    return (
        feats,
        row_grads.reshape(1, 1, rows, E),
        project_t.transpose(0, 2, 1),
        output_g,
        mix_g,
        gain_g,
    )


def solution(mesh):
    placed = (
        P("dp", "mp", None, None),
        P("dp", "mp", None),
        P(),
        P(),
        P(None, "dp", None),
        P(None, "dp", None),
        P(None, "dp", None),
        P(None, "dp"),
        P(("dp", "mp"), None, None),
    )
    return jax.shard_map(
        per_device,
        mesh=mesh,
        in_specs=placed,
        out_specs=(
            P(("dp", "mp"), None, None),
            P("dp", "mp", None, None),
            P(None, "dp", None),
            P(None, "dp", None),
            P(None, "dp", None),
            P(None, "dp"),
        ),
        check_vma=False,
    )
```

```python
import functools

import jax
import jax.numpy as jnp
from jax import lax
from jax.experimental import pallas as pl
from jax.experimental.pallas import tpu as pltpu
from jax.sharding import PartitionSpec as P

F = 512
E = 128
K = 32
LAYERS = 2
SAMP_DEV = 8
PAIR = 4
PW = PAIR * E
PAIRS = SAMP_DEV // PAIR
CHUNK = 128
EPS = 1e-05
MIB = 1024 * 1024
FULL, WHOLE, PART = 63.5, 58, 46
PIECE = 144
BF = jnp.bfloat16
F32 = jnp.float32


def params(mib):
    return pltpu.CompilerParams(vmem_limit_bytes=int(mib * MIB))


def dot(left, right):
    return jnp.dot(left, right, preferred_element_type=F32)


def dot_nt(left, right):
    return lax.dot_general(left, right, (((1,), (1,)), ((), ())), preferred_element_type=F32)


def dot_tn(left, right):
    return lax.dot_general(left, right, (((0,), (0,)), ((), ())), preferred_element_type=F32)


class Copies:
    def __init__(self, sems):
        self.sems, self.used, self.open = sems, 0, {}

    def start(self, key, source, target):
        copy = pltpu.make_async_copy(source, target, self.sems.at[self.used])
        self.used += 1
        copy.start()
        self.open[key] = copy

    def wait(self, *keys):
        for key in keys:
            if key in self.open:
                self.open.pop(key).wait()

    def drain(self):
        self.wait(*list(self.open))


BLOCK = 128
HBM = pl.BlockSpec(memory_space=pltpu.HBM)
VMEM = pl.BlockSpec(memory_space=pltpu.VMEM)


def pool_kernel(ids_ref, rows_ref, out_ref):
    bags, rows = out_ref.shape[0], rows_ref.shape[0]
    for low in range(0, bags, BLOCK):
        high = min(low + BLOCK + rows - bags, rows)
        bag = lax.broadcasted_iota(jnp.int32, (BLOCK, high - low), 0) + low
        hot = jnp.where(ids_ref[:, low:high] == bag, 1.0, 0.0).astype(BF)
        out_ref[low : low + BLOCK, :] = dot(hot, rows_ref[low:high, :]).astype(BF)


def pool(ids, rows, bags):
    return pl.pallas_call(
        pool_kernel,
        out_shape=jax.ShapeDtypeStruct((bags, E), BF),
        compiler_params=params(WHOLE),
        name="pool",
    )(ids, rows)


def expand_kernel(ids_ref, bags_ref, out_ref, table):
    rows, bags = out_ref.shape[0], bags_ref.shape[0]
    table[...] = jnp.zeros_like(table)
    for part in range(rows // BLOCK):
        table[part : part + 1, :] = ids_ref[:, part * BLOCK : (part + 1) * BLOCK]
    columns = table[...].T
    for part in range(rows // BLOCK):
        low = part * BLOCK
        first = max(low - (rows - bags), 0)
        last = min(low + BLOCK, bags)
        bag = lax.broadcasted_iota(jnp.int32, (BLOCK, last - first), 1) + first
        hot = jnp.where(columns[:, part : part + 1] == bag, 1.0, 0.0).astype(BF)
        out_ref[low : low + BLOCK, :] = dot(hot, bags_ref[first:last, :]).astype(BF)


def expand(ids, owner, rows):
    return pl.pallas_call(
        expand_kernel,
        out_shape=jax.ShapeDtypeStruct((rows, E), BF),
        scratch_shapes=[pltpu.VMEM((BLOCK, BLOCK), jnp.int32)],
        compiler_params=params(PART),
        name="expand",
    )(ids, owner)


def prepare_kernel(pos_ref, slot_ref, expo_ref, *refs, halves):
    weights, outs = refs[: 4 * halves], refs[4 * halves :]
    projects, outputs, mixes, gains = (weights[n * halves : (n + 1) * halves] for n in range(4))
    left_ref, back_ref, diag_ref, project_ref, gain_ref, scale_ref, perm_ref, unperm_ref = outs
    first = pos_ref[0] == 0

    def joined(parts, axis):
        if halves == 1:
            return parts[0]
        return jnp.where(
            first, jnp.concatenate(parts, axis=axis), jnp.concatenate(parts[::-1], axis=axis)
        )

    for layer in range(LAYERS):
        for half in range(halves):
            size = F // halves
            start = 0 if halves == 1 else pl.multiple_of((pos_ref[0] ^ half) * size, size)
            left_ref[layer, pl.ds(start, size), :] = mixes[half][layer]
        back_ref[layer] = left_ref[layer, :F, :].T
        project_t = joined([ref[layer] for ref in projects], 1)
        left_ref[layer, F:, :] = project_t
        none = jnp.zeros((E - K, F), BF)
        project_ref[layer] = jnp.concatenate([project_t, none], axis=0).T
        row = joined([ref[layer].astype(F32) for ref in outputs], 0).astype(BF)
        diag_ref[layer] = jnp.zeros((PAIR * K, PW), BF)
        for t in range(PAIR):
            diag_ref[layer, t * K : (t + 1) * K, t * E : (t + 1) * E] = row
    gain_ref[...] = joined([ref[...].astype(F32) for ref in gains], 1)
    expo = expo_ref[...]
    small = jnp.where(
        expo == 0, 0.25, jnp.where(expo == 1, 0.5, jnp.where(expo == 2, 1.0, 2.0))
    ).astype(BF)
    blocks = expo.shape[0]
    spread = jnp.where(
        lax.broadcasted_iota(jnp.int32, (blocks, E), 1) // (E // blocks)
        == lax.broadcasted_iota(jnp.int32, (blocks, E), 0),
        1.0,
        0.0,
    ).astype(BF)
    scale_ref[...] = dot_tn(small, spread)
    hot = jnp.where(slot_ref[...] == lax.broadcasted_iota(jnp.int32, (F, F), 0), 1.0, 0.0)
    perm_ref[...] = hot.astype(BF)
    unperm_ref[...] = hot.T.astype(BF)


def prepare(pos, slot_feature, block_exponent, weights):
    halves = len(weights[0])
    flat = [part for parts in weights for part in parts]
    return pl.pallas_call(
        functools.partial(prepare_kernel, halves=halves),
        out_shape=(
            jax.ShapeDtypeStruct((LAYERS, F + K, F), BF),
            jax.ShapeDtypeStruct((LAYERS, F, F), BF),
            jax.ShapeDtypeStruct((LAYERS, PAIR * K, PW), BF),
            jax.ShapeDtypeStruct((LAYERS, F, E), BF),
            jax.ShapeDtypeStruct((LAYERS, E), F32),
            jax.ShapeDtypeStruct((F, E), F32),
            jax.ShapeDtypeStruct((F, F), BF),
            jax.ShapeDtypeStruct((F, F), BF),
        ),
        in_specs=[pl.BlockSpec(memory_space=pltpu.SMEM)] + [VMEM] * (2 + len(flat)),
        out_specs=(VMEM,) * 8,
        compiler_params=params(FULL),
        name="prepare",
    )(pos, slot_feature.reshape(1, F), block_exponent.T, *flat)


def unslot(block, f_dev):
    if f_dev % 16:
        block = block.astype(F32)
    parts = [block[:, t * f_dev : (t + 1) * f_dev, :].reshape(F, E) for t in range(PAIR)]
    return jnp.concatenate(parts, axis=1).astype(BF)


CONSTANTS = ("perm", "scale", "left", "diag", "back", "project", "unperm")


def layers_kernel(pos_ref, gain_ref, recv_hbm, cot_hbm, *refs, f_dev, packed):
    sources, refs = dict(zip(CONSTANTS, refs)), refs[len(CONSTANTS) :]
    feats_hbm, slots_hbm = refs[:2]
    grads = 2 if packed else 4
    grad_outs, refs = refs[2 : 2 + grads], refs[2 + grads :]
    held, refs = dict(zip(CONSTANTS, refs)), refs[len(CONSTANTS) :]
    recv_ref, cot_ref, feats_ref, slots_ref = refs[:4]
    grad_refs, refs = refs[4 : 4 + grads], refs[4 + grads :]
    xs, ts, normed_s, inv_s, grad_s, next_s, wacc, gacc, dm, pj, ex, sems = refs
    left_ref, back_ref, diag_ref = held["left"], held["back"], held["diag"]
    project_ref, scale_ref = held["project"], held["scale"]
    copies = Copies(sems)

    def slot_rows(p):
        return slice(p * PAIR * f_dev, (p + 1) * PAIR * f_dev)

    def fetch(name):
        copies.start(name, sources[name], held[name])

    copies.start("recv", recv_hbm, recv_ref)
    for name in ("perm", "scale", "left", "diag"):
        fetch(name)
    copies.start("cot", cot_hbm, cot_ref)
    for name in ("back", "project", "unperm"):
        fetch(name)

    wacc[...] = jnp.zeros_like(wacc)
    gacc[...] = jnp.zeros_like(gacc)

    def pair_steps(p):
        columns = slice(p * PW, (p + 1) * PW)
        x = dot(held["perm"][...], unslot(recv_ref[:, slot_rows(p)], f_dev))
        scale = scale_ref[...]
        x = (x * jnp.concatenate([scale] * PAIR, axis=1)).astype(BF)
        yield
        same = (
            lax.broadcasted_iota(jnp.int32, (PAIR * K, PW), 0) // K
            == lax.broadcasted_iota(jnp.int32, (PAIR * K, PW), 1) // E
        )
        saved = []
        for layer in range(LAYERS):
            xs[layer, :, columns] = x
            mixed = dot(left_ref[layer], x)
            projected = jnp.concatenate([mixed[F:]] * PAIR, axis=0)
            projected = jnp.where(same, projected, 0.0).astype(BF)
            paired = dot_nt(x, projected).astype(BF)
            low = dot(paired, diag_ref[layer])
            gain = gain_ref[layer : layer + 1, :]
            saved.append((x, projected, paired))
            yield
            for t in range(PAIR):
                lanes = slice(t * E, (t + 1) * E)
                for r in range(0, F, CHUNK):
                    rows = slice(r, r + CHUNK)
                    total = x[rows, lanes].astype(F32) + mixed[rows, lanes] + low[rows, lanes]
                    centred = total - jnp.sum(total, axis=-1, keepdims=True) * (1.0 / E)
                    variance = jnp.sum(centred * centred, axis=-1, keepdims=True) * (1.0 / E)
                    inverse = lax.rsqrt(variance + EPS)
                    normed = centred * inverse
                    normed_s[p, layer, rows, lanes] = normed
                    inv_s[p, layer, rows, lanes] = jnp.broadcast_to(inverse, (CHUNK, E))
                    out = (normed * gain).astype(BF)
                    if layer == LAYERS - 1:
                        feats_ref[p * PAIR + t, rows, :] = out
                    else:
                        next_s[p, rows, lanes] = out
            yield
            x = next_s[p]

        for layer in reversed(range(LAYERS)):
            x, projected, paired = saved[layer]
            gain = gain_ref[layer : layer + 1, :]
            dgain = jnp.zeros((8, E), F32)
            for t in range(PAIR):
                lanes = slice(t * E, (t + 1) * E)
                for r in range(0, F, CHUNK):
                    rows = slice(r, r + CHUNK)
                    if layer == LAYERS - 1:
                        upper = cot_ref[p * PAIR + t, rows, :].astype(F32)
                    else:
                        upper = next_s[p, rows, lanes].astype(F32)
                    normed = normed_s[p, layer, rows, lanes]
                    dgain = dgain + jnp.sum((upper * normed).reshape(CHUNK // 8, 8, E), axis=0)
                    scaled = upper * gain
                    first = jnp.sum(scaled, axis=-1, keepdims=True) * (1.0 / E)
                    second = jnp.sum(scaled * normed, axis=-1, keepdims=True) * (1.0 / E)
                    total = inv_s[p, layer, rows, lanes] * (scaled - first - normed * second)
                    grad_s[p, rows, lanes] = total
                    next_s[p, rows, lanes] = total.astype(BF)
            gacc[layer] += dgain
            yield
            total_low = next_s[p]
            ts[layer, :F, columns] = total_low
            grad_paired = dot_nt(total_low, diag_ref[layer]).astype(BF)
            wide = dot_tn(grad_paired, x)
            grad_projected = jnp.concatenate(
                [wide[t * K : (t + 1) * K, t * E : (t + 1) * E] for t in range(PAIR)], axis=1
            ).astype(BF)
            ts[layer, F:, columns] = grad_projected
            wide = dot_tn(paired, total_low)
            for t in range(PAIR):
                wacc[layer] += wide[t * K : (t + 1) * K, t * E : (t + 1) * E]
            rest = jnp.zeros((E - K, PW), BF)
            upstream = dot(back_ref[layer], total_low) + dot(
                jnp.concatenate([grad_paired, project_ref[layer]], axis=1),
                jnp.concatenate([projected, grad_projected, rest], axis=0),
            )
            yield
            for t in range(PAIR):
                lanes = slice(t * E, (t + 1) * E)
                for r in range(0, F, CHUNK):
                    rows = slice(r, r + CHUNK)
                    out = (grad_s[p, rows, lanes] + upstream[rows, lanes]).astype(BF)
                    if layer == 0:
                        out = (out.astype(F32) * scale_ref[rows]).astype(BF)
                    next_s[p, rows, lanes] = out

        slots = dot(held["unperm"][...], next_s[p])
        if f_dev % 16 == 0:
            slots = slots.astype(BF)
        for t in range(PAIR):
            low = (p * PAIR + t) * f_dev
            slots_ref[:, low : low + f_dev, :] = (
                slots[:, t * E : (t + 1) * E].reshape(F // f_dev, f_dev, E).astype(BF)
            )
        yield

    def weight_grads(layer):
        dm[layer] = dot_nt(ts[layer], xs[layer])
        gain_row = jnp.sum(gacc[layer], axis=0, keepdims=True)
        if not packed:
            mix_ref, project_t_ref, output_ref, gain_out_ref = grad_refs
            mix_ref[layer] = dm[layer, :F, :]
            project_t_ref[layer] = dm[layer, F:, :]
            output_ref[layer] = wacc[layer]
            gain_out_ref[layer : layer + 1, :] = gain_row
            return
        half = F // 2
        for d in range(2):
            for q in range(8):
                low = d * half + (q // 4) * E
                pj[d, layer * 8 + q] = dm[
                    layer, F + 8 * (q % 4) : F + 8 * (q % 4) + 8, low : low + E
                ]
                if q < 2:
                    low = d * (K // 2) + 8 * q
                    ex[d, layer * 8 + q] = wacc[layer, low : low + 8, :]
                else:
                    row = gain_row[:, d * 64 : (d + 1) * 64]
                    ex[d, layer * 8 + q] = jnp.broadcast_to(
                        jnp.concatenate([row, row], axis=1), (8, E)
                    )
        my_d, my_m = pos_ref[0], pos_ref[1]
        flip = (my_m >> 3) ^ layer
        for core in range(2):
            for rx in range(2):
                for ry in range(2):
                    for low_z in range(2):
                        q = (my_m & 7) ^ (low_z * 4 + rx * 2 + core)
                        d = my_d ^ ry
                        start = pl.multiple_of(d * half + q * 32, 32)
                        block = dm[layer, pl.ds(start, 32), :]
                        pieces = [block[:, c * E : (c + 1) * E] for c in range(4)]
                        pieces += [pj[d, layer * 8 + q], ex[d, layer * 8 + q]]
                        place = (rx * 2 + ry) * 4 + low_z + 2 * flip
                        grad_refs[core][place] = jnp.concatenate(pieces, axis=0).astype(BF)

    programs = [pair_steps(p) for p in range(PAIRS)]
    phases = 4 * LAYERS + 2
    for tick in range(phases):
        if tick == 0:
            copies.wait("recv", "perm", "scale")
        if tick == 1:
            copies.wait("left", "diag")
        if tick == 2 * LAYERS + 1:
            copies.wait("cot", "back", "project", "unperm")
        if tick == 2 * LAYERS + 1:
            copies.start("feats", feats_ref, feats_hbm)
        for program in programs:
            next(program)
        for layer in reversed(range(LAYERS)):
            if tick == phases - 1 - 2 * layer:
                weight_grads(layer)
    copies.start("slots", slots_ref, slots_hbm)
    for n in range(grads):
        copies.start(("grad", n), grad_refs[n], grad_outs[n])
    copies.drain()


def run_layers(pos, recv, cotangent, operands, f_dev, packed):
    left, back, diag, project, gain, scale, perm, unperm = operands
    tables = F // f_dev

    def shape(dims, dtype=F32):
        return jax.ShapeDtypeStruct(dims, dtype)

    if packed:
        grads = [shape((16, PIECE, E), BF)] * 2
    else:
        grads = [
            shape((LAYERS, F, F)),
            shape((LAYERS, K, F)),
            shape((LAYERS, K, E)),
            shape((LAYERS, E)),
        ]
    given = dict(
        perm=perm, scale=scale, left=left, diag=diag, back=back, project=project, unperm=unperm
    )
    constants = [given[name] for name in CONSTANTS]
    width = SAMP_DEV * E
    big = [shape((SAMP_DEV, F, E), BF), shape((tables, SAMP_DEV * f_dev, E), BF)]
    outs = big + grads

    def scratch(x):
        return pltpu.VMEM(x.shape, x.dtype)

    copies = len(constants) + 4 + len(grads)
    return pl.pallas_call(
        functools.partial(layers_kernel, f_dev=f_dev, packed=packed),
        out_shape=outs,
        in_specs=[pl.BlockSpec(memory_space=pltpu.SMEM), VMEM]
        + [HBM] * (2 + len(constants)),
        out_specs=[HBM] * len(outs),
        scratch_shapes=[scratch(x) for x in constants]
        + [scratch(recv), scratch(cotangent)]
        + [scratch(x) for x in outs]
        + [
            pltpu.VMEM((LAYERS, F, width), BF),
            pltpu.VMEM((LAYERS, F + K, width), BF),
            pltpu.VMEM((PAIRS, LAYERS, F, PW), F32),
            pltpu.VMEM((PAIRS, LAYERS, F, PW), F32),
            pltpu.VMEM((PAIRS, F, PW), F32),
            pltpu.VMEM((PAIRS, F, PW), BF),
            pltpu.VMEM((LAYERS, K, E), F32),
            pltpu.VMEM((LAYERS, 8, E), F32),
            pltpu.VMEM((LAYERS, F + K, F), F32),
            pltpu.VMEM((2, 16, 8, E), F32),
            pltpu.VMEM((2, 16, 8, E), F32),
            pltpu.SemaphoreType.DMA((copies,)),
        ],
        compiler_params=params(WHOLE),
        name="layers",
    )(pos, gain, recv, cotangent, *constants)


def across(x, d, m):
    pairs = [(i, i ^ (d * 16 + m)) for i in range(32)]
    return lax.ppermute(x, ("dp", "mp"), pairs)


def added(parts):
    return sum(part.astype(F32) for part in parts).astype(BF)


def finish_kernel(pos_ref, *refs, factor):
    parts = refs[:4]
    mix_ref, project_ref, output_ref, gain_ref, pj, ex = refs[4:]
    my_m = pos_ref[1]
    for c in range(2):
        for rx in range(2):
            for rz in range(4):
                m = my_m ^ (rz * 4 + rx * 2 + c)
                piece = parts[c * 2 + rx][rz].astype(F32) * factor
                start = pl.multiple_of((m & 7) * 32, 32)
                for n in range(4):
                    mix_ref[m >> 3, pl.ds(start, 32), n * E : (n + 1) * E] = piece[
                        n * 32 : (n + 1) * 32
                    ]
                pj[m] = piece[128:136]
                ex[m] = piece[136:144]
    for l in range(LAYERS):
        for h in range(2):
            for b in range(4):
                project_ref[l, b * 8 : (b + 1) * 8, h * E : (h + 1) * E] = pj[l * 8 + h * 4 + b]
        for b in range(2):
            output_ref[l, b * 8 : (b + 1) * 8, :] = ex[l * 8 + b]
        gain_ref[l : l + 1, :] = ex[l * 8 + 2][0:1, :64]


def finish(pos, parts, factor):
    return pl.pallas_call(
        functools.partial(finish_kernel, factor=factor),
        out_shape=[
            jax.ShapeDtypeStruct((LAYERS, F // 2, F), F32),
            jax.ShapeDtypeStruct((LAYERS, K, F // 2), F32),
            jax.ShapeDtypeStruct((LAYERS, K // 2, E), F32),
            jax.ShapeDtypeStruct((LAYERS, E // 2), F32),
        ],
        in_specs=[pl.BlockSpec(memory_space=pltpu.SMEM)] + [VMEM] * 4,
        out_specs=[VMEM] * 4,
        scratch_shapes=[pltpu.VMEM((16, 8, E), F32)] * 2,
        compiler_params=params(PART),
        name="finish",
    )(pos, *parts)


def exchange(x):
    return lax.all_to_all(x, "mp", split_axis=0, concat_axis=0, tiled=True)


def return_packed(pos, slots, keep, send, ids, factor):
    rows, bags = ids.shape[1], slots.shape[0] * slots.shape[1]
    other = across(send, 0, 1)
    own, to_y, to_x, to_xy = [
        added([part[4 * r : 4 * r + 4] for part in (keep, other)]) for r in range(4)
    ]
    parts = [own, across(to_y, 1, 0), across(to_x, 0, 2), across(to_xy, 1, 2)]
    owner = exchange(slots)
    quarters = [added([part[r : r + 1] for part in parts]) for r in range(4)]
    parts = [quarters[0]] + [across(quarters[r], 0, 4 * r) for r in range(1, 4)]
    piece = added(parts)
    column = jnp.concatenate([piece] + [across(piece, 0, 4 * r) for r in range(1, 4)], axis=0)
    column, owner = lax.optimization_barrier((column, owner))
    beside = across(column, 0, 2)
    row_grads = expand(ids, owner.reshape(bags, E), rows)
    beside, row_grads = lax.optimization_barrier((beside, row_grads))
    parts = [column, beside, across(column, 0, 1), across(beside, 0, 1)]
    parts, row_grads = lax.optimization_barrier((parts, row_grads))
    return row_grads, finish(pos, parts, factor)


def per_device(
    table_rows,
    bag_ids,
    slot_feature,
    block_exponent,
    fm_project,
    fm_output,
    mix_weight,
    norm_gain,
    out_cotangent,
):
    tables, groups = lax.axis_size("mp"), lax.axis_size("dp")
    f_dev = F // tables
    bags = SAMP_DEV * tables * f_dev
    rows = table_rows.shape[2]
    ids = bag_ids.reshape(1, rows)
    factor = 1.0 / float(SAMP_DEV * tables * groups) ** 0.5
    pos = jnp.stack([lax.axis_index("dp"), lax.axis_index("mp")]).astype(jnp.int32)

    pooled = pool(ids, table_rows.reshape(rows, E), bags).reshape(tables, SAMP_DEV * f_dev, E)
    recv = exchange(pooled)
    weights = (fm_project.transpose(0, 2, 1), fm_output, mix_weight, norm_gain)
    if groups == 2:
        weights = [(part, lax.ppermute(part, "dp", [(0, 1), (1, 0)])) for part in weights]
    else:
        weights = [
            (lax.all_gather(part, "dp", axis=axis, tiled=True),)
            for part, axis in zip(weights, (2, 1, 1, 1))
        ]
    operands = prepare(pos, slot_feature, block_exponent, weights)
    packed = (groups, tables) == (2, 16)
    feats, slots, *grads = run_layers(pos, recv, out_cotangent, operands, f_dev, packed)
    if packed:
        row_grads, shares = return_packed(pos, slots, *grads, ids, factor)
        project_t, output_g, mix_g, gain_g = shares[1], shares[2], shares[0], shares[3]
    else:
        row_grads = expand(ids, exchange(slots).reshape(bags, E), rows)
        mix_g, project_t, output_g, gain_g = (
            lax.psum_scatter(part.astype(BF), "dp", scatter_dimension=axis, tiled=True).astype(F32)
            * factor
            for part, axis in zip(lax.psum(tuple(grads), "mp"), (1, 2, 1, 1))
        )
    return (
        feats,
        row_grads.reshape(1, 1, rows, E),
        project_t.transpose(0, 2, 1),
        output_g,
        mix_g,
        gain_g,
    )


def solution(mesh):
    placed = (
        P("dp", "mp", None, None),
        P("dp", "mp", None),
        P(),
        P(),
        P(None, "dp", None),
        P(None, "dp", None),
        P(None, "dp", None),
        P(None, "dp"),
        P(("dp", "mp"), None, None),
    )
    return jax.shard_map(
        per_device,
        mesh=mesh,
        in_specs=placed,
        out_specs=(
            P(("dp", "mp"), None, None),
            P("dp", "mp", None, None),
            P(None, "dp", None),
            P(None, "dp", None),
            P(None, "dp", None),
            P(None, "dp"),
        ),
        check_vma=False,
    )
```

```python
import functools

import jax
import jax.numpy as jnp
from jax import lax
from jax.experimental import pallas as pl
from jax.experimental.pallas import tpu as pltpu
from jax.sharding import PartitionSpec as P

F = 512
E = 128
K = 32
LAYERS = 2
SAMP_DEV = 8
PAIR = 4
PW = PAIR * E
PAIRS = SAMP_DEV // PAIR
CHUNK = 128
EPS = 1e-05
MIB = 1024 * 1024
FULL, WHOLE, PART = 63.5, 58, 46
PIECE = 144
BF = jnp.bfloat16
F32 = jnp.float32


def params(mib):
    return pltpu.CompilerParams(vmem_limit_bytes=int(mib * MIB))


def dot(left, right):
    return jnp.dot(left, right, preferred_element_type=F32)


def dot_nt(left, right):
    return lax.dot_general(left, right, (((1,), (1,)), ((), ())), preferred_element_type=F32)


def dot_tn(left, right):
    return lax.dot_general(left, right, (((0,), (0,)), ((), ())), preferred_element_type=F32)


class Copies:
    def __init__(self, sems):
        self.sems, self.used, self.open = sems, 0, {}

    def start(self, key, source, target):
        copy = pltpu.make_async_copy(source, target, self.sems.at[self.used])
        self.used += 1
        copy.start()
        self.open[key] = copy

    def wait(self, *keys):
        for key in keys:
            if key in self.open:
                self.open.pop(key).wait()

    def drain(self):
        self.wait(*list(self.open))


BLOCK = 128
HBM = pl.BlockSpec(memory_space=pltpu.HBM)
VMEM = pl.BlockSpec(memory_space=pltpu.VMEM)


def pool_kernel(ids_ref, rows_ref, out_ref):
    bags, rows = out_ref.shape[0], rows_ref.shape[0]
    for low in range(0, bags, BLOCK):
        high = min(low + BLOCK + rows - bags, rows)
        bag = lax.broadcasted_iota(jnp.int32, (BLOCK, high - low), 0) + low
        hot = jnp.where(ids_ref[:, low:high] == bag, 1.0, 0.0).astype(BF)
        out_ref[low : low + BLOCK, :] = dot(hot, rows_ref[low:high, :]).astype(BF)


def pool(ids, rows, bags):
    return pl.pallas_call(
        pool_kernel,
        out_shape=jax.ShapeDtypeStruct((bags, E), BF),
        compiler_params=params(WHOLE),
        name="pool",
    )(ids, rows)


def expand_kernel(ids_ref, bags_ref, out_ref, table):
    rows, bags = out_ref.shape[0], bags_ref.shape[0]
    table[...] = jnp.zeros_like(table)
    for part in range(rows // BLOCK):
        table[part : part + 1, :] = ids_ref[:, part * BLOCK : (part + 1) * BLOCK]
    columns = table[...].T
    for part in range(rows // BLOCK):
        low = part * BLOCK
        first = max(low - (rows - bags), 0)
        last = min(low + BLOCK, bags)
        bag = lax.broadcasted_iota(jnp.int32, (BLOCK, last - first), 1) + first
        hot = jnp.where(columns[:, part : part + 1] == bag, 1.0, 0.0).astype(BF)
        out_ref[low : low + BLOCK, :] = dot(hot, bags_ref[first:last, :]).astype(BF)


def expand(ids, owner, rows):
    return pl.pallas_call(
        expand_kernel,
        out_shape=jax.ShapeDtypeStruct((rows, E), BF),
        scratch_shapes=[pltpu.VMEM((BLOCK, BLOCK), jnp.int32)],
        compiler_params=params(PART),
        name="expand",
    )(ids, owner)


def prepare_kernel(pos_ref, slot_ref, expo_ref, *refs, halves):
    weights, outs = refs[: 4 * halves], refs[4 * halves :]
    projects, outputs, mixes, gains = (weights[n * halves : (n + 1) * halves] for n in range(4))
    left_ref, back_ref, diag_ref, project_ref, gain_ref, scale_ref, perm_ref, unperm_ref = outs
    first = pos_ref[0] == 0

    def joined(parts, axis):
        if halves == 1:
            return parts[0]
        return jnp.where(
            first, jnp.concatenate(parts, axis=axis), jnp.concatenate(parts[::-1], axis=axis)
        )

    for layer in range(LAYERS):
        for half in range(halves):
            size = F // halves
            start = 0 if halves == 1 else pl.multiple_of((pos_ref[0] ^ half) * size, size)
            left_ref[layer, pl.ds(start, size), :] = mixes[half][layer]
        back_ref[layer] = left_ref[layer, :F, :].T
        project_t = joined([ref[layer] for ref in projects], 1)
        left_ref[layer, F:, :] = project_t
        none = jnp.zeros((E - K, F), BF)
        project_ref[layer] = jnp.concatenate([project_t, none], axis=0).T
        row = joined([ref[layer].astype(F32) for ref in outputs], 0).astype(BF)
        diag_ref[layer] = jnp.zeros((PAIR * K, PW), BF)
        for t in range(PAIR):
            diag_ref[layer, t * K : (t + 1) * K, t * E : (t + 1) * E] = row
    gain_ref[...] = joined([ref[...].astype(F32) for ref in gains], 1)
    expo = expo_ref[...]
    small = jnp.where(
        expo == 0, 0.25, jnp.where(expo == 1, 0.5, jnp.where(expo == 2, 1.0, 2.0))
    ).astype(BF)
    blocks = expo.shape[0]
    spread = jnp.where(
        lax.broadcasted_iota(jnp.int32, (blocks, E), 1) // (E // blocks)
        == lax.broadcasted_iota(jnp.int32, (blocks, E), 0),
        1.0,
        0.0,
    ).astype(BF)
    scale_ref[...] = dot_tn(small, spread)
    hot = jnp.where(slot_ref[...] == lax.broadcasted_iota(jnp.int32, (F, F), 0), 1.0, 0.0)
    perm_ref[...] = hot.astype(BF)
    unperm_ref[...] = hot.T.astype(BF)


def prepare(pos, slot_feature, block_exponent, weights):
    halves = len(weights[0])
    flat = [part for parts in weights for part in parts]
    return pl.pallas_call(
        functools.partial(prepare_kernel, halves=halves),
        out_shape=(
            jax.ShapeDtypeStruct((LAYERS, F + K, F), BF),
            jax.ShapeDtypeStruct((LAYERS, F, F), BF),
            jax.ShapeDtypeStruct((LAYERS, PAIR * K, PW), BF),
            jax.ShapeDtypeStruct((LAYERS, F, E), BF),
            jax.ShapeDtypeStruct((LAYERS, E), F32),
            jax.ShapeDtypeStruct((F, E), F32),
            jax.ShapeDtypeStruct((F, F), BF),
            jax.ShapeDtypeStruct((F, F), BF),
        ),
        in_specs=[pl.BlockSpec(memory_space=pltpu.SMEM)] + [VMEM] * (2 + len(flat)),
        out_specs=(VMEM,) * 8,
        compiler_params=params(FULL),
        name="prepare",
    )(pos, slot_feature.reshape(1, F), block_exponent.T, *flat)


def unslot(block, f_dev):
    if f_dev % 16:
        block = block.astype(F32)
    parts = [block[:, t * f_dev : (t + 1) * f_dev, :].reshape(F, E) for t in range(PAIR)]
    return jnp.concatenate(parts, axis=1).astype(BF)


CONSTANTS = ("perm", "scale", "left", "diag", "back", "project", "unperm")


def layers_kernel(pos_ref, gain_ref, recv_hbm, cot_hbm, *refs, f_dev, packed):
    sources, refs = dict(zip(CONSTANTS, refs)), refs[len(CONSTANTS) :]
    feats_hbm, slots_hbm = refs[:2]
    grads = 2 if packed else 4
    grad_outs, refs = refs[2 : 2 + grads], refs[2 + grads :]
    held, refs = dict(zip(CONSTANTS, refs)), refs[len(CONSTANTS) :]
    recv_ref, cot_ref, feats_ref, slots_ref = refs[:4]
    grad_refs, refs = refs[4 : 4 + grads], refs[4 + grads :]
    xs, ts, normed_s, inv_s, grad_s, next_s, wacc, gacc, dm, pj, ex, sems = refs
    left_ref, back_ref, diag_ref = held["left"], held["back"], held["diag"]
    project_ref, scale_ref = held["project"], held["scale"]
    copies = Copies(sems)

    def slot_rows(p):
        return slice(p * PAIR * f_dev, (p + 1) * PAIR * f_dev)

    def fetch(name):
        copies.start(name, sources[name], held[name])

    copies.start("recv", recv_hbm, recv_ref)
    for name in ("perm", "scale", "left", "diag"):
        fetch(name)
    copies.start("cot", cot_hbm, cot_ref)
    for name in ("back", "project", "unperm"):
        fetch(name)

    wacc[...] = jnp.zeros_like(wacc)
    gacc[...] = jnp.zeros_like(gacc)

    def pair_steps(p):
        columns = slice(p * PW, (p + 1) * PW)
        x = dot(held["perm"][...], unslot(recv_ref[:, slot_rows(p)], f_dev))
        scale = scale_ref[...]
        x = (x * jnp.concatenate([scale] * PAIR, axis=1)).astype(BF)
        yield
        same = (
            lax.broadcasted_iota(jnp.int32, (PAIR * K, PW), 0) // K
            == lax.broadcasted_iota(jnp.int32, (PAIR * K, PW), 1) // E
        )
        saved = []
        for layer in range(LAYERS):
            xs[layer, :, columns] = x
            projected = dot(left_ref[layer, F:], x)
            projected = jnp.concatenate([projected] * PAIR, axis=0)
            projected = jnp.where(same, projected, 0.0).astype(BF)
            paired = dot_nt(x, projected).astype(BF)
            mixed = dot(
                jnp.concatenate([left_ref[layer, :F], paired], axis=1),
                jnp.concatenate([x, diag_ref[layer]], axis=0),
            )
            gain = gain_ref[layer : layer + 1, :]
            saved.append((x, projected, paired))
            yield
            for t in range(PAIR):
                lanes = slice(t * E, (t + 1) * E)
                for r in range(0, F, CHUNK):
                    rows = slice(r, r + CHUNK)
                    total = x[rows, lanes].astype(F32) + mixed[rows, lanes]
                    centred = total - jnp.sum(total, axis=-1, keepdims=True) * (1.0 / E)
                    variance = jnp.sum(centred * centred, axis=-1, keepdims=True) * (1.0 / E)
                    inverse = lax.rsqrt(variance + EPS)
                    normed = centred * inverse
                    normed_s[p, layer, rows, lanes] = normed
                    inv_s[p, layer, rows, lanes] = jnp.broadcast_to(inverse, (CHUNK, E))
                    out = (normed * gain).astype(BF)
                    if layer == LAYERS - 1:
                        feats_ref[p * PAIR + t, rows, :] = out
                    else:
                        next_s[p, rows, lanes] = out
            yield
            x = next_s[p]

        for layer in reversed(range(LAYERS)):
            x, projected, paired = saved[layer]
            gain = gain_ref[layer : layer + 1, :]
            dgain = jnp.zeros((8, E), F32)
            for t in range(PAIR):
                lanes = slice(t * E, (t + 1) * E)
                for r in range(0, F, CHUNK):
                    rows = slice(r, r + CHUNK)
                    if layer == LAYERS - 1:
                        upper = cot_ref[p * PAIR + t, rows, :].astype(F32)
                    else:
                        upper = next_s[p, rows, lanes].astype(F32)
                    normed = normed_s[p, layer, rows, lanes]
                    dgain = dgain + jnp.sum((upper * normed).reshape(CHUNK // 8, 8, E), axis=0)
                    scaled = upper * gain
                    first = jnp.sum(scaled, axis=-1, keepdims=True) * (1.0 / E)
                    second = jnp.sum(scaled * normed, axis=-1, keepdims=True) * (1.0 / E)
                    total = inv_s[p, layer, rows, lanes] * (scaled - first - normed * second)
                    grad_s[p, rows, lanes] = total
                    next_s[p, rows, lanes] = total.astype(BF)
            gacc[layer] += dgain
            yield
            total_low = next_s[p]
            ts[layer, :F, columns] = total_low
            grad_paired = dot_nt(total_low, diag_ref[layer]).astype(BF)
            wide = dot_tn(grad_paired, x)
            grad_projected = jnp.concatenate(
                [wide[t * K : (t + 1) * K, t * E : (t + 1) * E] for t in range(PAIR)], axis=1
            ).astype(BF)
            ts[layer, F:, columns] = grad_projected
            wide = dot_tn(paired, total_low)
            for t in range(PAIR):
                wacc[layer] += wide[t * K : (t + 1) * K, t * E : (t + 1) * E]
            rest = jnp.zeros((E - K, PW), BF)
            upstream = dot(
                jnp.concatenate([back_ref[layer], grad_paired, project_ref[layer]], axis=1),
                jnp.concatenate([total_low, projected, grad_projected, rest], axis=0),
            )
            yield
            for t in range(PAIR):
                lanes = slice(t * E, (t + 1) * E)
                for r in range(0, F, CHUNK):
                    rows = slice(r, r + CHUNK)
                    out = grad_s[p, rows, lanes] + upstream[rows, lanes]
                    out = (out * scale_ref[rows] if layer == 0 else out).astype(BF)
                    next_s[p, rows, lanes] = out

        slots = dot(held["unperm"][...], next_s[p])
        if f_dev % 16 == 0:
            slots = slots.astype(BF)
        for t in range(PAIR):
            low = (p * PAIR + t) * f_dev
            slots_ref[:, low : low + f_dev, :] = (
                slots[:, t * E : (t + 1) * E].reshape(F // f_dev, f_dev, E).astype(BF)
            )
        yield

    def weight_grads(layer):
        dm[layer] = dot_nt(ts[layer], xs[layer])
        gain_row = jnp.sum(gacc[layer], axis=0, keepdims=True)
        if not packed:
            mix_ref, project_t_ref, output_ref, gain_out_ref = grad_refs
            mix_ref[layer] = dm[layer, :F, :]
            project_t_ref[layer] = dm[layer, F:, :]
            output_ref[layer] = wacc[layer]
            gain_out_ref[layer : layer + 1, :] = gain_row
            return
        half = F // 2
        for d in range(2):
            for q in range(8):
                low = d * half + (q // 4) * E
                pj[d, layer * 8 + q] = dm[
                    layer, F + 8 * (q % 4) : F + 8 * (q % 4) + 8, low : low + E
                ]
                if q < 2:
                    low = d * (K // 2) + 8 * q
                    ex[d, layer * 8 + q] = wacc[layer, low : low + 8, :]
                else:
                    row = gain_row[:, d * 64 : (d + 1) * 64]
                    ex[d, layer * 8 + q] = jnp.broadcast_to(
                        jnp.concatenate([row, row], axis=1), (8, E)
                    )
        my_d, my_m = pos_ref[0], pos_ref[1]
        flip = (my_m >> 3) ^ layer
        for core in range(2):
            for rx in range(2):
                for ry in range(2):
                    for low_z in range(2):
                        q = (my_m & 7) ^ (low_z * 4 + rx * 2 + core)
                        d = my_d ^ ry
                        start = pl.multiple_of(d * half + q * 32, 32)
                        block = dm[layer, pl.ds(start, 32), :]
                        pieces = [block[:, c * E : (c + 1) * E] for c in range(4)]
                        pieces += [pj[d, layer * 8 + q], ex[d, layer * 8 + q]]
                        place = (rx * 2 + ry) * 4 + low_z + 2 * flip
                        grad_refs[core][place] = jnp.concatenate(pieces, axis=0).astype(BF)

    programs = [pair_steps(p) for p in range(PAIRS)]
    phases = 4 * LAYERS + 2
    for tick in range(phases):
        if tick == 0:
            copies.wait("recv", "perm", "scale")
        if tick == 1:
            copies.wait("left", "diag")
        if tick == 2 * LAYERS + 1:
            copies.wait("cot", "back", "project", "unperm")
        if tick == 2 * LAYERS + 1:
            copies.start("feats", feats_ref, feats_hbm)
        for program in programs:
            next(program)
        for layer in reversed(range(LAYERS)):
            if tick == phases - 1 - 2 * layer:
                weight_grads(layer)
    copies.start("slots", slots_ref, slots_hbm)
    for n in range(grads):
        copies.start(("grad", n), grad_refs[n], grad_outs[n])
    copies.drain()


def run_layers(pos, recv, cotangent, operands, f_dev, packed):
    left, back, diag, project, gain, scale, perm, unperm = operands
    tables = F // f_dev

    def shape(dims, dtype=F32):
        return jax.ShapeDtypeStruct(dims, dtype)

    if packed:
        grads = [shape((16, PIECE, E), BF)] * 2
    else:
        grads = [
            shape((LAYERS, F, F)),
            shape((LAYERS, K, F)),
            shape((LAYERS, K, E)),
            shape((LAYERS, E)),
        ]
    given = dict(
        perm=perm, scale=scale, left=left, diag=diag, back=back, project=project, unperm=unperm
    )
    constants = [given[name] for name in CONSTANTS]
    width = SAMP_DEV * E
    big = [shape((SAMP_DEV, F, E), BF), shape((tables, SAMP_DEV * f_dev, E), BF)]
    outs = big + grads

    def scratch(x):
        return pltpu.VMEM(x.shape, x.dtype)

    copies = len(constants) + 4 + len(grads)
    return pl.pallas_call(
        functools.partial(layers_kernel, f_dev=f_dev, packed=packed),
        out_shape=outs,
        in_specs=[pl.BlockSpec(memory_space=pltpu.SMEM), VMEM]
        + [HBM] * (2 + len(constants)),
        out_specs=[HBM] * len(outs),
        scratch_shapes=[scratch(x) for x in constants]
        + [scratch(recv), scratch(cotangent)]
        + [scratch(x) for x in outs]
        + [
            pltpu.VMEM((LAYERS, F, width), BF),
            pltpu.VMEM((LAYERS, F + K, width), BF),
            pltpu.VMEM((PAIRS, LAYERS, F, PW), F32),
            pltpu.VMEM((PAIRS, LAYERS, F, PW), F32),
            pltpu.VMEM((PAIRS, F, PW), F32),
            pltpu.VMEM((PAIRS, F, PW), BF),
            pltpu.VMEM((LAYERS, K, E), F32),
            pltpu.VMEM((LAYERS, 8, E), F32),
            pltpu.VMEM((LAYERS, F + K, F), F32),
            pltpu.VMEM((2, 16, 8, E), F32),
            pltpu.VMEM((2, 16, 8, E), F32),
            pltpu.SemaphoreType.DMA((copies,)),
        ],
        compiler_params=params(WHOLE),
        name="layers",
    )(pos, gain, recv, cotangent, *constants)


def across(x, d, m):
    pairs = [(i, i ^ (d * 16 + m)) for i in range(32)]
    return lax.ppermute(x, ("dp", "mp"), pairs)


def added(parts):
    return sum(part.astype(F32) for part in parts).astype(BF)


def finish_kernel(pos_ref, *refs, factor):
    parts = refs[:4]
    mix_ref, project_ref, output_ref, gain_ref, pj, ex = refs[4:]
    my_m = pos_ref[1]
    for c in range(2):
        for rx in range(2):
            for rz in range(4):
                m = my_m ^ (rz * 4 + rx * 2 + c)
                piece = parts[c * 2 + rx][rz].astype(F32) * factor
                start = pl.multiple_of((m & 7) * 32, 32)
                for n in range(4):
                    mix_ref[m >> 3, pl.ds(start, 32), n * E : (n + 1) * E] = piece[
                        n * 32 : (n + 1) * 32
                    ]
                pj[m] = piece[128:136]
                ex[m] = piece[136:144]
    for l in range(LAYERS):
        for h in range(2):
            for b in range(4):
                project_ref[l, b * 8 : (b + 1) * 8, h * E : (h + 1) * E] = pj[l * 8 + h * 4 + b]
        for b in range(2):
            output_ref[l, b * 8 : (b + 1) * 8, :] = ex[l * 8 + b]
        gain_ref[l : l + 1, :] = ex[l * 8 + 2][0:1, :64]


def finish(pos, parts, factor):
    return pl.pallas_call(
        functools.partial(finish_kernel, factor=factor),
        out_shape=[
            jax.ShapeDtypeStruct((LAYERS, F // 2, F), F32),
            jax.ShapeDtypeStruct((LAYERS, K, F // 2), F32),
            jax.ShapeDtypeStruct((LAYERS, K // 2, E), F32),
            jax.ShapeDtypeStruct((LAYERS, E // 2), F32),
        ],
        in_specs=[pl.BlockSpec(memory_space=pltpu.SMEM)] + [VMEM] * 4,
        out_specs=[VMEM] * 4,
        scratch_shapes=[pltpu.VMEM((16, 8, E), F32)] * 2,
        compiler_params=params(PART),
        name="finish",
    )(pos, *parts)


def exchange(x):
    return lax.all_to_all(x, "mp", split_axis=0, concat_axis=0, tiled=True)


def return_packed(pos, slots, keep, send, ids, factor):
    rows, bags = ids.shape[1], slots.shape[0] * slots.shape[1]
    other = across(send, 0, 1)
    own, to_y, to_x, to_xy = [
        added([part[4 * r : 4 * r + 4] for part in (keep, other)]) for r in range(4)
    ]
    parts = [own, across(to_y, 1, 0), across(to_x, 0, 2), across(to_xy, 1, 2)]
    owner = exchange(slots)
    quarters = [added([part[r : r + 1] for part in parts]) for r in range(4)]
    parts = [quarters[0]] + [across(quarters[r], 0, 4 * r) for r in range(1, 4)]
    piece = added(parts)
    column = jnp.concatenate([piece] + [across(piece, 0, 4 * r) for r in range(1, 4)], axis=0)
    column, owner = lax.optimization_barrier((column, owner))
    beside = across(column, 0, 2)
    row_grads = expand(ids, owner.reshape(bags, E), rows)
    beside, row_grads = lax.optimization_barrier((beside, row_grads))
    parts = [column, beside, across(column, 0, 1), across(beside, 0, 1)]
    parts, row_grads = lax.optimization_barrier((parts, row_grads))
    return row_grads, finish(pos, parts, factor)


def per_device(
    table_rows,
    bag_ids,
    slot_feature,
    block_exponent,
    fm_project,
    fm_output,
    mix_weight,
    norm_gain,
    out_cotangent,
):
    tables, groups = lax.axis_size("mp"), lax.axis_size("dp")
    f_dev = F // tables
    bags = SAMP_DEV * tables * f_dev
    rows = table_rows.shape[2]
    ids = bag_ids.reshape(1, rows)
    factor = 1.0 / float(SAMP_DEV * tables * groups) ** 0.5
    pos = jnp.stack([lax.axis_index("dp"), lax.axis_index("mp")]).astype(jnp.int32)

    pooled = pool(ids, table_rows.reshape(rows, E), bags).reshape(tables, SAMP_DEV * f_dev, E)
    recv = exchange(pooled)
    weights = (fm_project.transpose(0, 2, 1), fm_output, mix_weight, norm_gain)
    if groups == 2:
        weights = [(part, lax.ppermute(part, "dp", [(0, 1), (1, 0)])) for part in weights]
    else:
        weights = [
            (lax.all_gather(part, "dp", axis=axis, tiled=True),)
            for part, axis in zip(weights, (2, 1, 1, 1))
        ]
    operands = prepare(pos, slot_feature, block_exponent, weights)
    packed = (groups, tables) == (2, 16)
    feats, slots, *grads = run_layers(pos, recv, out_cotangent, operands, f_dev, packed)
    if packed:
        row_grads, shares = return_packed(pos, slots, *grads, ids, factor)
        project_t, output_g, mix_g, gain_g = shares[1], shares[2], shares[0], shares[3]
    else:
        row_grads = expand(ids, exchange(slots).reshape(bags, E), rows)
        mix_g, project_t, output_g, gain_g = (
            lax.psum_scatter(part.astype(BF), "dp", scatter_dimension=axis, tiled=True).astype(F32)
            * factor
            for part, axis in zip(lax.psum(tuple(grads), "mp"), (1, 2, 1, 1))
        )
    return (
        feats,
        row_grads.reshape(1, 1, rows, E),
        project_t.transpose(0, 2, 1),
        output_g,
        mix_g,
        gain_g,
    )


def solution(mesh):
    placed = (
        P("dp", "mp", None, None),
        P("dp", "mp", None),
        P(),
        P(),
        P(None, "dp", None),
        P(None, "dp", None),
        P(None, "dp", None),
        P(None, "dp"),
        P(("dp", "mp"), None, None),
    )
    return jax.shard_map(
        per_device,
        mesh=mesh,
        in_specs=placed,
        out_specs=(
            P(("dp", "mp"), None, None),
            P("dp", "mp", None, None),
            P(None, "dp", None),
            P(None, "dp", None),
            P(None, "dp", None),
            P(None, "dp"),
        ),
        check_vma=False,
    )
```

```python
import functools

import jax
import jax.numpy as jnp
from jax import lax
from jax.experimental import pallas as pl
from jax.experimental.pallas import tpu as pltpu
from jax.sharding import PartitionSpec as P

F = 512
E = 128
K = 32
LAYERS = 2
SAMP_DEV = 8
PAIR = 4
PW = PAIR * E
PAIRS = SAMP_DEV // PAIR
CHUNK = 128
EPS = 1e-05
MIB = 1024 * 1024
FULL, WHOLE, PART = 63.5, 58, 46
PIECE = 144
BF = jnp.bfloat16
F32 = jnp.float32


def params(mib):
    return pltpu.CompilerParams(vmem_limit_bytes=int(mib * MIB))


def dot(left, right):
    return jnp.dot(left, right, preferred_element_type=F32)


def dot_nt(left, right):
    return lax.dot_general(left, right, (((1,), (1,)), ((), ())), preferred_element_type=F32)


def dot_tn(left, right):
    return lax.dot_general(left, right, (((0,), (0,)), ((), ())), preferred_element_type=F32)


class Copies:
    def __init__(self, sems):
        self.sems, self.used, self.open = sems, 0, {}

    def start(self, key, source, target):
        copy = pltpu.make_async_copy(source, target, self.sems.at[self.used])
        self.used += 1
        copy.start()
        self.open[key] = copy

    def wait(self, *keys):
        for key in keys:
            if key in self.open:
                self.open.pop(key).wait()

    def drain(self):
        self.wait(*list(self.open))


BLOCK = 128
HBM = pl.BlockSpec(memory_space=pltpu.HBM)
VMEM = pl.BlockSpec(memory_space=pltpu.VMEM)


def pool_kernel(ids_ref, rows_ref, out_ref):
    bags, rows = out_ref.shape[0], rows_ref.shape[0]
    for low in range(0, bags, BLOCK):
        high = min(low + BLOCK + rows - bags, rows)
        bag = lax.broadcasted_iota(jnp.int32, (BLOCK, high - low), 0) + low
        hot = jnp.where(ids_ref[:, low:high] == bag, 1.0, 0.0).astype(BF)
        out_ref[low : low + BLOCK, :] = dot(hot, rows_ref[low:high, :]).astype(BF)


def pool(ids, rows, bags):
    return pl.pallas_call(
        pool_kernel,
        out_shape=jax.ShapeDtypeStruct((bags, E), BF),
        compiler_params=params(WHOLE),
        name="pool",
    )(ids, rows)


def expand_kernel(ids_ref, bags_ref, out_ref, table):
    rows, bags = out_ref.shape[0], bags_ref.shape[0]
    table[...] = jnp.zeros_like(table)
    for part in range(rows // BLOCK):
        table[part : part + 1, :] = ids_ref[:, part * BLOCK : (part + 1) * BLOCK]
    columns = table[...].T
    for part in range(rows // BLOCK):
        low = part * BLOCK
        first = max(low - (rows - bags), 0)
        last = min(low + BLOCK, bags)
        bag = lax.broadcasted_iota(jnp.int32, (BLOCK, last - first), 1) + first
        hot = jnp.where(columns[:, part : part + 1] == bag, 1.0, 0.0).astype(BF)
        out_ref[low : low + BLOCK, :] = dot(hot, bags_ref[first:last, :]).astype(BF)


def expand(ids, owner, rows):
    return pl.pallas_call(
        expand_kernel,
        out_shape=jax.ShapeDtypeStruct((rows, E), BF),
        scratch_shapes=[pltpu.VMEM((BLOCK, BLOCK), jnp.int32)],
        compiler_params=params(PART),
        name="expand",
    )(ids, owner)


def prepare_kernel(pos_ref, slot_ref, expo_ref, *refs, halves):
    weights, outs = refs[: 4 * halves], refs[4 * halves :]
    projects, outputs, mixes, gains = (weights[n * halves : (n + 1) * halves] for n in range(4))
    left_ref, back_ref, diag_ref, project_ref, gain_ref, scale_ref, unperm_ref = outs
    first = pos_ref[0] == 0

    def joined(parts, axis):
        if halves == 1:
            return parts[0]
        return jnp.where(
            first, jnp.concatenate(parts, axis=axis), jnp.concatenate(parts[::-1], axis=axis)
        )

    for layer in range(LAYERS):
        for half in range(halves):
            size = F // halves
            start = 0 if halves == 1 else pl.multiple_of((pos_ref[0] ^ half) * size, size)
            left_ref[layer, pl.ds(start, size), :] = mixes[half][layer]
        back_ref[layer] = left_ref[layer, :F, :].T
        project_t = joined([ref[layer] for ref in projects], 1)
        left_ref[layer, F:, :] = project_t
        none = jnp.zeros((E - K, F), BF)
        project_ref[layer] = jnp.concatenate([project_t, none], axis=0).T
        row = joined([ref[layer].astype(F32) for ref in outputs], 0).astype(BF)
        diag_ref[layer] = jnp.zeros((PAIR * K, PW), BF)
        for t in range(PAIR):
            diag_ref[layer, t * K : (t + 1) * K, t * E : (t + 1) * E] = row
    gain_ref[...] = joined([ref[...].astype(F32) for ref in gains], 1)
    expo = expo_ref[...]
    small = jnp.where(
        expo == 0, 0.25, jnp.where(expo == 1, 0.5, jnp.where(expo == 2, 1.0, 2.0))
    ).astype(BF)
    blocks = expo.shape[0]
    spread = jnp.where(
        lax.broadcasted_iota(jnp.int32, (blocks, E), 1) // (E // blocks)
        == lax.broadcasted_iota(jnp.int32, (blocks, E), 0),
        1.0,
        0.0,
    ).astype(BF)
    scale_ref[...] = dot_tn(small, spread)
    hot = jnp.where(slot_ref[...] == lax.broadcasted_iota(jnp.int32, (F, F), 0), 1.0, 0.0)
    unperm_ref[...] = hot.T.astype(BF)


def prepare(pos, slot_feature, block_exponent, weights):
    halves = len(weights[0])
    flat = [part for parts in weights for part in parts]
    return pl.pallas_call(
        functools.partial(prepare_kernel, halves=halves),
        out_shape=(
            jax.ShapeDtypeStruct((LAYERS, F + K, F), BF),
            jax.ShapeDtypeStruct((LAYERS, F, F), BF),
            jax.ShapeDtypeStruct((LAYERS, PAIR * K, PW), BF),
            jax.ShapeDtypeStruct((LAYERS, F, E), BF),
            jax.ShapeDtypeStruct((LAYERS, E), F32),
            jax.ShapeDtypeStruct((F, E), F32),
            jax.ShapeDtypeStruct((F, F), BF),
        ),
        in_specs=[pl.BlockSpec(memory_space=pltpu.SMEM)] + [VMEM] * (2 + len(flat)),
        out_specs=(VMEM,) * 7,
        compiler_params=params(FULL),
        name="prepare",
    )(pos, slot_feature.reshape(1, F), block_exponent.T, *flat)


def unslot(block, f_dev):
    if f_dev % 16:
        block = block.astype(F32)
    parts = [block[:, t * f_dev : (t + 1) * f_dev, :].reshape(F, E) for t in range(PAIR)]
    return jnp.concatenate(parts, axis=1).astype(BF)


CONSTANTS = ("scale", "left", "diag", "back", "project", "unperm")


def layers_kernel(pos_ref, gain_ref, slot_ref, recv_hbm, cot_hbm, *refs, f_dev, packed):
    sources, refs = dict(zip(CONSTANTS, refs)), refs[len(CONSTANTS) :]
    feats_hbm, slots_hbm = refs[:2]
    grads = 2 if packed else 4
    grad_outs, refs = refs[2 : 2 + grads], refs[2 + grads :]
    held, refs = dict(zip(CONSTANTS, refs)), refs[len(CONSTANTS) :]
    recv_ref, cot_ref, feats_ref, slots_ref = refs[:4]
    grad_refs, refs = refs[4 : 4 + grads], refs[4 + grads :]
    xs, ts, normed_s, inv_s, grad_s, next_s, wacc, gacc, dm, pj, ex, sems = refs
    left_ref, back_ref, diag_ref = held["left"], held["back"], held["diag"]
    project_ref, scale_ref = held["project"], held["scale"]
    copies = Copies(sems)

    def slot_rows(p):
        return slice(p * PAIR * f_dev, (p + 1) * PAIR * f_dev)

    def fetch(name):
        copies.start(name, sources[name], held[name])

    copies.start("recv", recv_hbm, recv_ref)
    for name in ("scale", "left", "diag"):
        fetch(name)
    copies.start("cot", cot_hbm, cot_ref)
    for name in ("back", "project", "unperm"):
        fetch(name)
    hot = slot_ref[...] == lax.broadcasted_iota(jnp.int32, (F, F), 0)
    perm = jnp.where(hot, 1.0, 0.0).astype(BF)

    wacc[...] = jnp.zeros_like(wacc)
    gacc[...] = jnp.zeros_like(gacc)

    def pair_steps(p):
        columns = slice(p * PW, (p + 1) * PW)
        x = dot(perm, unslot(recv_ref[:, slot_rows(p)], f_dev))
        scale = scale_ref[...]
        x = (x * jnp.concatenate([scale] * PAIR, axis=1)).astype(BF)
        yield
        same = (
            lax.broadcasted_iota(jnp.int32, (PAIR * K, PW), 0) // K
            == lax.broadcasted_iota(jnp.int32, (PAIR * K, PW), 1) // E
        )
        saved = []
        for layer in range(LAYERS):
            xs[layer, :, columns] = x
            projected = dot(left_ref[layer, F:], x)
            projected = jnp.concatenate([projected] * PAIR, axis=0)
            projected = jnp.where(same, projected, 0.0).astype(BF)
            paired = dot_nt(x, projected).astype(BF)
            mixed = dot(
                jnp.concatenate([left_ref[layer, :F], paired], axis=1),
                jnp.concatenate([x, diag_ref[layer]], axis=0),
            )
            gain = gain_ref[layer : layer + 1, :]
            saved.append((x, projected, paired))
            yield
            for t in range(PAIR):
                lanes = slice(t * E, (t + 1) * E)
                for r in range(0, F, CHUNK):
                    rows = slice(r, r + CHUNK)
                    total = x[rows, lanes].astype(F32) + mixed[rows, lanes]
                    centred = total - jnp.sum(total, axis=-1, keepdims=True) * (1.0 / E)
                    variance = jnp.sum(centred * centred, axis=-1, keepdims=True) * (1.0 / E)
                    inverse = lax.rsqrt(variance + EPS)
                    normed = centred * inverse
                    normed_s[p, layer, rows, lanes] = normed
                    inv_s[p, layer, rows, lanes] = jnp.broadcast_to(inverse, (CHUNK, E))
                    out = (normed * gain).astype(BF)
                    if layer == LAYERS - 1:
                        feats_ref[p * PAIR + t, rows, :] = out
                    else:
                        next_s[p, rows, lanes] = out
            yield
            x = next_s[p]

        for layer in reversed(range(LAYERS)):
            x, projected, paired = saved[layer]
            gain = gain_ref[layer : layer + 1, :]
            dgain = jnp.zeros((8, E), F32)
            for t in range(PAIR):
                lanes = slice(t * E, (t + 1) * E)
                for r in range(0, F, CHUNK):
                    rows = slice(r, r + CHUNK)
                    if layer == LAYERS - 1:
                        upper = cot_ref[p * PAIR + t, rows, :].astype(F32)
                    else:
                        upper = next_s[p, rows, lanes].astype(F32)
                    normed = normed_s[p, layer, rows, lanes]
                    dgain = dgain + jnp.sum((upper * normed).reshape(CHUNK // 8, 8, E), axis=0)
                    scaled = upper * gain
                    first = jnp.sum(scaled, axis=-1, keepdims=True) * (1.0 / E)
                    second = jnp.sum(scaled * normed, axis=-1, keepdims=True) * (1.0 / E)
                    total = inv_s[p, layer, rows, lanes] * (scaled - first - normed * second)
                    grad_s[p, rows, lanes] = total
                    next_s[p, rows, lanes] = total.astype(BF)
            gacc[layer] += dgain
            yield
            total_low = next_s[p]
            ts[layer, :F, columns] = total_low
            grad_paired = dot_nt(total_low, diag_ref[layer]).astype(BF)
            wide = dot_tn(grad_paired, x)
            grad_projected = jnp.concatenate(
                [wide[t * K : (t + 1) * K, t * E : (t + 1) * E] for t in range(PAIR)], axis=1
            ).astype(BF)
            ts[layer, F:, columns] = grad_projected
            wide = dot_tn(paired, total_low)
            for t in range(PAIR):
                wacc[layer] += wide[t * K : (t + 1) * K, t * E : (t + 1) * E]
            rest = jnp.zeros((E - K, PW), BF)
            upstream = dot(
                jnp.concatenate([back_ref[layer], grad_paired, project_ref[layer]], axis=1),
                jnp.concatenate([total_low, projected, grad_projected, rest], axis=0),
            )
            yield
            for t in range(PAIR):
                lanes = slice(t * E, (t + 1) * E)
                for r in range(0, F, CHUNK):
                    rows = slice(r, r + CHUNK)
                    out = grad_s[p, rows, lanes] + upstream[rows, lanes]
                    out = (out * scale_ref[rows] if layer == 0 else out).astype(BF)
                    next_s[p, rows, lanes] = out

        slots = dot(held["unperm"][...], next_s[p])
        if f_dev % 16 == 0:
            slots = slots.astype(BF)
        for t in range(PAIR):
            low = (p * PAIR + t) * f_dev
            slots_ref[:, low : low + f_dev, :] = (
                slots[:, t * E : (t + 1) * E].reshape(F // f_dev, f_dev, E).astype(BF)
            )
        yield

    def weight_grads(layer):
        dm[layer] = dot_nt(ts[layer], xs[layer])
        gain_row = jnp.sum(gacc[layer], axis=0, keepdims=True)
        if not packed:
            mix_ref, project_t_ref, output_ref, gain_out_ref = grad_refs
            mix_ref[layer] = dm[layer, :F, :]
            project_t_ref[layer] = dm[layer, F:, :]
            output_ref[layer] = wacc[layer]
            gain_out_ref[layer : layer + 1, :] = gain_row
            return
        half = F // 2
        for d in range(2):
            for q in range(8):
                low = d * half + (q // 4) * E
                pj[d, layer * 8 + q] = dm[
                    layer, F + 8 * (q % 4) : F + 8 * (q % 4) + 8, low : low + E
                ]
                if q < 2:
                    low = d * (K // 2) + 8 * q
                    ex[d, layer * 8 + q] = wacc[layer, low : low + 8, :]
                else:
                    row = gain_row[:, d * 64 : (d + 1) * 64]
                    ex[d, layer * 8 + q] = jnp.broadcast_to(
                        jnp.concatenate([row, row], axis=1), (8, E)
                    )
        my_d, my_m = pos_ref[0], pos_ref[1]
        flip = (my_m >> 3) ^ layer
        for core in range(2):
            for rx in range(2):
                for ry in range(2):
                    for low_z in range(2):
                        q = (my_m & 7) ^ (low_z * 4 + rx * 2 + core)
                        d = my_d ^ ry
                        start = pl.multiple_of(d * half + q * 32, 32)
                        block = dm[layer, pl.ds(start, 32), :]
                        pieces = [block[:, c * E : (c + 1) * E] for c in range(4)]
                        pieces += [pj[d, layer * 8 + q], ex[d, layer * 8 + q]]
                        place = (rx * 2 + ry) * 4 + low_z + 2 * flip
                        grad_refs[core][place] = jnp.concatenate(pieces, axis=0).astype(BF)

    programs = [pair_steps(p) for p in range(PAIRS)]
    phases = 4 * LAYERS + 2
    for tick in range(phases):
        if tick == 0:
            copies.wait("recv", "scale")
        if tick == 1:
            copies.wait("left", "diag")
        if tick == 2 * LAYERS + 1:
            copies.wait("cot", "back", "project", "unperm")
        if tick == 2 * LAYERS + 1:
            copies.start("feats", feats_ref, feats_hbm)
        for program in programs:
            next(program)
        for layer in reversed(range(LAYERS)):
            if tick == phases - 1 - 2 * layer:
                weight_grads(layer)
    copies.start("slots", slots_ref, slots_hbm)
    for n in range(grads):
        copies.start(("grad", n), grad_refs[n], grad_outs[n])
    copies.drain()


def run_layers(pos, slot_feature, recv, cotangent, operands, f_dev, packed):
    left, back, diag, project, gain, scale, unperm = operands
    tables = F // f_dev

    def shape(dims, dtype=F32):
        return jax.ShapeDtypeStruct(dims, dtype)

    if packed:
        grads = [shape((16, PIECE, E), BF)] * 2
    else:
        grads = [
            shape((LAYERS, F, F)),
            shape((LAYERS, K, F)),
            shape((LAYERS, K, E)),
            shape((LAYERS, E)),
        ]
    given = dict(
        scale=scale, left=left, diag=diag, back=back, project=project, unperm=unperm
    )
    constants = [given[name] for name in CONSTANTS]
    width = SAMP_DEV * E
    big = [shape((SAMP_DEV, F, E), BF), shape((tables, SAMP_DEV * f_dev, E), BF)]
    outs = big + grads

    def scratch(x):
        return pltpu.VMEM(x.shape, x.dtype)

    copies = len(constants) + 4 + len(grads)
    return pl.pallas_call(
        functools.partial(layers_kernel, f_dev=f_dev, packed=packed),
        out_shape=outs,
        in_specs=[pl.BlockSpec(memory_space=pltpu.SMEM), VMEM, VMEM]
        + [HBM] * (2 + len(constants)),
        out_specs=[HBM] * len(outs),
        scratch_shapes=[scratch(x) for x in constants]
        + [scratch(recv), scratch(cotangent)]
        + [scratch(x) for x in outs]
        + [
            pltpu.VMEM((LAYERS, F, width), BF),
            pltpu.VMEM((LAYERS, F + K, width), BF),
            pltpu.VMEM((PAIRS, LAYERS, F, PW), F32),
            pltpu.VMEM((PAIRS, LAYERS, F, PW), F32),
            pltpu.VMEM((PAIRS, F, PW), F32),
            pltpu.VMEM((PAIRS, F, PW), BF),
            pltpu.VMEM((LAYERS, K, E), F32),
            pltpu.VMEM((LAYERS, 8, E), F32),
            pltpu.VMEM((LAYERS, F + K, F), F32),
            pltpu.VMEM((2, 16, 8, E), F32),
            pltpu.VMEM((2, 16, 8, E), F32),
            pltpu.SemaphoreType.DMA((copies,)),
        ],
        compiler_params=params(WHOLE),
        name="layers",
    )(pos, gain, slot_feature.reshape(1, F), recv, cotangent, *constants)


def across(x, d, m):
    pairs = [(i, i ^ (d * 16 + m)) for i in range(32)]
    return lax.ppermute(x, ("dp", "mp"), pairs)


def added(parts):
    return sum(part.astype(F32) for part in parts).astype(BF)


def finish_kernel(pos_ref, *refs, factor):
    parts = refs[:4]
    mix_ref, project_ref, output_ref, gain_ref, pj, ex = refs[4:]
    my_m = pos_ref[1]
    for c in range(2):
        for rx in range(2):
            for rz in range(4):
                m = my_m ^ (rz * 4 + rx * 2 + c)
                piece = parts[c * 2 + rx][rz].astype(F32) * factor
                start = pl.multiple_of((m & 7) * 32, 32)
                for n in range(4):
                    mix_ref[m >> 3, pl.ds(start, 32), n * E : (n + 1) * E] = piece[
                        n * 32 : (n + 1) * 32
                    ]
                pj[m] = piece[128:136]
                ex[m] = piece[136:144]
    for l in range(LAYERS):
        for h in range(2):
            for b in range(4):
                project_ref[l, b * 8 : (b + 1) * 8, h * E : (h + 1) * E] = pj[l * 8 + h * 4 + b]
        for b in range(2):
            output_ref[l, b * 8 : (b + 1) * 8, :] = ex[l * 8 + b]
        gain_ref[l : l + 1, :] = ex[l * 8 + 2][0:1, :64]


def finish(pos, parts, factor):
    return pl.pallas_call(
        functools.partial(finish_kernel, factor=factor),
        out_shape=[
            jax.ShapeDtypeStruct((LAYERS, F // 2, F), F32),
            jax.ShapeDtypeStruct((LAYERS, K, F // 2), F32),
            jax.ShapeDtypeStruct((LAYERS, K // 2, E), F32),
            jax.ShapeDtypeStruct((LAYERS, E // 2), F32),
        ],
        in_specs=[pl.BlockSpec(memory_space=pltpu.SMEM)] + [VMEM] * 4,
        out_specs=[VMEM] * 4,
        scratch_shapes=[pltpu.VMEM((16, 8, E), F32)] * 2,
        compiler_params=params(PART),
        name="finish",
    )(pos, *parts)


def exchange(x):
    return lax.all_to_all(x, "mp", split_axis=0, concat_axis=0, tiled=True)


def return_packed(pos, slots, keep, send, ids, factor):
    rows, bags = ids.shape[1], slots.shape[0] * slots.shape[1]
    other = across(send, 0, 1)
    both = [part.reshape(2, 2, 4, PIECE, E) for part in (keep, other)]
    to_y, own = (added([part[:, ry] for part in both]) for ry in (1, 0))
    both = [own, across(to_y, 1, 0)]
    to_x, own = (added([part[rx] for part in both]) for rx in (1, 0))
    parts = [own, across(to_x, 0, 2)]
    owner = exchange(slots)
    quarters = [added([part[r : r + 1] for part in parts]) for r in range(4)]
    parts = [quarters[0]] + [across(quarters[r], 0, 4 * r) for r in range(1, 4)]
    piece = added(parts)
    column = jnp.concatenate([piece] + [across(piece, 0, 4 * r) for r in range(1, 4)], axis=0)
    column, owner = lax.optimization_barrier((column, owner))
    beside = across(column, 0, 2)
    row_grads = expand(ids, owner.reshape(bags, E), rows)
    beside, row_grads = lax.optimization_barrier((beside, row_grads))
    parts = [column, beside, across(column, 0, 1), across(beside, 0, 1)]
    parts, row_grads = lax.optimization_barrier((parts, row_grads))
    return row_grads, finish(pos, parts, factor)


def per_device(
    table_rows,
    bag_ids,
    slot_feature,
    block_exponent,
    fm_project,
    fm_output,
    mix_weight,
    norm_gain,
    out_cotangent,
):
    tables, groups = lax.axis_size("mp"), lax.axis_size("dp")
    f_dev = F // tables
    bags = SAMP_DEV * tables * f_dev
    rows = table_rows.shape[2]
    ids = bag_ids.reshape(1, rows)
    factor = 1.0 / float(SAMP_DEV * tables * groups) ** 0.5
    pos = jnp.stack([lax.axis_index("dp"), lax.axis_index("mp")]).astype(jnp.int32)

    pooled = pool(ids, table_rows.reshape(rows, E), bags).reshape(tables, SAMP_DEV * f_dev, E)
    recv = exchange(pooled)
    weights = (fm_project.transpose(0, 2, 1), fm_output, mix_weight, norm_gain)
    if groups == 2:
        weights = [(part, lax.ppermute(part, "dp", [(0, 1), (1, 0)])) for part in weights]
    else:
        weights = [
            (lax.all_gather(part, "dp", axis=axis, tiled=True),)
            for part, axis in zip(weights, (2, 1, 1, 1))
        ]
    operands = prepare(pos, slot_feature, block_exponent, weights)
    packed = (groups, tables) == (2, 16)
    feats, slots, *grads = run_layers(pos, slot_feature, recv, out_cotangent, operands, f_dev, packed)
    if packed:
        row_grads, shares = return_packed(pos, slots, *grads, ids, factor)
        project_t, output_g, mix_g, gain_g = shares[1], shares[2], shares[0], shares[3]
    else:
        row_grads = expand(ids, exchange(slots).reshape(bags, E), rows)
        mix_g, project_t, output_g, gain_g = (
            lax.psum_scatter(part.astype(BF), "dp", scatter_dimension=axis, tiled=True).astype(F32)
            * factor
            for part, axis in zip(lax.psum(tuple(grads), "mp"), (1, 2, 1, 1))
        )
    return (
        feats,
        row_grads.reshape(1, 1, rows, E),
        project_t.transpose(0, 2, 1),
        output_g,
        mix_g,
        gain_g,
    )


def solution(mesh):
    placed = (
        P("dp", "mp", None, None),
        P("dp", "mp", None),
        P(),
        P(),
        P(None, "dp", None),
        P(None, "dp", None),
        P(None, "dp", None),
        P(None, "dp"),
        P(("dp", "mp"), None, None),
    )
    return jax.shard_map(
        per_device,
        mesh=mesh,
        in_specs=placed,
        out_specs=(
            P(("dp", "mp"), None, None),
            P("dp", "mp", None, None),
            P(None, "dp", None),
            P(None, "dp", None),
            P(None, "dp", None),
            P(None, "dp"),
        ),
        check_vma=False,
    )
```

```python
import functools

import jax
import jax.numpy as jnp
from jax import lax
from jax.experimental import pallas as pl
from jax.experimental.pallas import tpu as pltpu
from jax.sharding import PartitionSpec as P

F = 512
E = 128
K = 32
LAYERS = 2
SAMP_DEV = 8
PAIR = 4
PW = PAIR * E
PAIRS = SAMP_DEV // PAIR
CHUNK = 128
EPS = 1e-05
MIB = 1024 * 1024
FULL, WHOLE, PART = 63.5, 58, 46
PIECE = 144
BF = jnp.bfloat16
F32 = jnp.float32


def params(mib):
    return pltpu.CompilerParams(vmem_limit_bytes=int(mib * MIB))


def dot(left, right):
    return jnp.dot(left, right, preferred_element_type=F32)


def dot_nt(left, right):
    return lax.dot_general(left, right, (((1,), (1,)), ((), ())), preferred_element_type=F32)


def dot_tn(left, right):
    return lax.dot_general(left, right, (((0,), (0,)), ((), ())), preferred_element_type=F32)


class Copies:
    def __init__(self, sems):
        self.sems, self.used, self.open = sems, 0, {}

    def start(self, key, source, target):
        copy = pltpu.make_async_copy(source, target, self.sems.at[self.used])
        self.used += 1
        copy.start()
        self.open[key] = copy

    def wait(self, *keys):
        for key in keys:
            if key in self.open:
                self.open.pop(key).wait()

    def drain(self):
        self.wait(*list(self.open))


BLOCK = 128
HBM = pl.BlockSpec(memory_space=pltpu.HBM)
VMEM = pl.BlockSpec(memory_space=pltpu.VMEM)


def pool_kernel(ids_ref, rows_ref, out_ref):
    bags, rows = out_ref.shape[0], rows_ref.shape[0]
    for low in range(0, bags, BLOCK):
        high = min(low + BLOCK + rows - bags, rows)
        bag = lax.broadcasted_iota(jnp.int32, (BLOCK, high - low), 0) + low
        hot = jnp.where(ids_ref[:, low:high] == bag, 1.0, 0.0).astype(BF)
        out_ref[low : low + BLOCK, :] = dot(hot, rows_ref[low:high, :]).astype(BF)


def pool(ids, rows, bags):
    return pl.pallas_call(
        pool_kernel,
        out_shape=jax.ShapeDtypeStruct((bags, E), BF),
        compiler_params=params(WHOLE),
        name="pool",
    )(ids, rows)


def expand_kernel(ids_ref, bags_ref, out_ref, table):
    rows, bags = out_ref.shape[0], bags_ref.shape[0]
    table[...] = jnp.zeros_like(table)
    for part in range(rows // BLOCK):
        table[part : part + 1, :] = ids_ref[:, part * BLOCK : (part + 1) * BLOCK]
    columns = table[...].T
    for part in range(rows // BLOCK):
        low = part * BLOCK
        first = max(low - (rows - bags), 0)
        last = min(low + BLOCK, bags)
        bag = lax.broadcasted_iota(jnp.int32, (BLOCK, last - first), 1) + first
        hot = jnp.where(columns[:, part : part + 1] == bag, 1.0, 0.0).astype(BF)
        out_ref[low : low + BLOCK, :] = dot(hot, bags_ref[first:last, :]).astype(BF)


def expand(ids, owner, rows):
    return pl.pallas_call(
        expand_kernel,
        out_shape=jax.ShapeDtypeStruct((rows, E), BF),
        scratch_shapes=[pltpu.VMEM((BLOCK, BLOCK), jnp.int32)],
        compiler_params=params(PART),
        name="expand",
    )(ids, owner)


def prepare_kernel(pos_ref, slot_ref, expo_ref, *refs, halves):
    weights, outs = refs[: 4 * halves], refs[4 * halves :]
    projects, outputs, mixes, gains = (weights[n * halves : (n + 1) * halves] for n in range(4))
    left_ref, back_ref, diag_ref, project_ref, gain_ref, scale_ref, unperm_ref = outs
    first = pos_ref[0] == 0

    def joined(parts, axis):
        if halves == 1:
            return parts[0]
        return jnp.where(
            first, jnp.concatenate(parts, axis=axis), jnp.concatenate(parts[::-1], axis=axis)
        )

    for layer in range(LAYERS):
        for half in range(halves):
            size = F // halves
            start = 0 if halves == 1 else pl.multiple_of((pos_ref[0] ^ half) * size, size)
            left_ref[layer, pl.ds(start, size), :] = mixes[half][layer]
        back_ref[layer] = left_ref[layer, :F, :].T
        project_t = joined([ref[layer] for ref in projects], 1)
        left_ref[layer, F:, :] = project_t
        none = jnp.zeros((E - K, F), BF)
        project_ref[layer] = jnp.concatenate([project_t, none], axis=0).T
        row = joined([ref[layer].astype(F32) for ref in outputs], 0).astype(BF)
        diag_ref[layer] = jnp.zeros((PAIR * K, PW), BF)
        for t in range(PAIR):
            diag_ref[layer, t * K : (t + 1) * K, t * E : (t + 1) * E] = row
    gain_ref[...] = joined([ref[...].astype(F32) for ref in gains], 1)
    expo = expo_ref[...]
    small = jnp.where(
        expo == 0, 0.25, jnp.where(expo == 1, 0.5, jnp.where(expo == 2, 1.0, 2.0))
    ).astype(BF)
    blocks = expo.shape[0]
    spread = jnp.where(
        lax.broadcasted_iota(jnp.int32, (blocks, E), 1) // (E // blocks)
        == lax.broadcasted_iota(jnp.int32, (blocks, E), 0),
        1.0,
        0.0,
    ).astype(BF)
    scale_ref[...] = dot_tn(small, spread)
    hot = jnp.where(slot_ref[...] == lax.broadcasted_iota(jnp.int32, (F, F), 0), 1.0, 0.0)
    unperm_ref[...] = hot.T.astype(BF)


def prepare(pos, slot_feature, block_exponent, weights):
    halves = len(weights[0])
    flat = [part for parts in weights for part in parts]
    return pl.pallas_call(
        functools.partial(prepare_kernel, halves=halves),
        out_shape=(
            jax.ShapeDtypeStruct((LAYERS, F + K, F), BF),
            jax.ShapeDtypeStruct((LAYERS, F, F), BF),
            jax.ShapeDtypeStruct((LAYERS, PAIR * K, PW), BF),
            jax.ShapeDtypeStruct((LAYERS, F, E), BF),
            jax.ShapeDtypeStruct((LAYERS, E), F32),
            jax.ShapeDtypeStruct((F, E), F32),
            jax.ShapeDtypeStruct((F, F), BF),
        ),
        in_specs=[pl.BlockSpec(memory_space=pltpu.SMEM)] + [VMEM] * (2 + len(flat)),
        out_specs=(VMEM,) * 7,
        compiler_params=params(FULL),
        name="prepare",
    )(pos, slot_feature.reshape(1, F), block_exponent.T, *flat)


def unslot(block, f_dev):
    if f_dev % 16:
        block = block.astype(F32)
    parts = [block[:, t * f_dev : (t + 1) * f_dev, :].reshape(F, E) for t in range(PAIR)]
    return jnp.concatenate(parts, axis=1).astype(BF)


CONSTANTS = ("scale", "left", "diag", "back", "project", "unperm")


def layers_kernel(pos_ref, gain_ref, slot_ref, recv_hbm, cot_hbm, *refs, f_dev, packed):
    sources, refs = dict(zip(CONSTANTS, refs)), refs[len(CONSTANTS) :]
    feats_hbm, slots_hbm = refs[:2]
    grads = 2 if packed else 4
    grad_outs, refs = refs[2 : 2 + grads], refs[2 + grads :]
    held, refs = dict(zip(CONSTANTS, refs)), refs[len(CONSTANTS) :]
    recv_ref, cot_ref, feats_ref, slots_ref = refs[:4]
    grad_refs, refs = refs[4 : 4 + grads], refs[4 + grads :]
    xs, ts, normed_s, inv_s, grad_s, next_s, wacc, gacc, dm, pj, ex, sems = refs
    left_ref, back_ref, diag_ref = held["left"], held["back"], held["diag"]
    project_ref, scale_ref = held["project"], held["scale"]
    copies = Copies(sems)

    def slot_rows(p):
        return slice(p * PAIR * f_dev, (p + 1) * PAIR * f_dev)

    def fetch(name):
        copies.start(name, sources[name], held[name])

    copies.start("recv", recv_hbm, recv_ref)
    for name in ("scale", "left", "diag"):
        fetch(name)
    copies.start("cot", cot_hbm, cot_ref)
    for name in ("back", "project", "unperm"):
        fetch(name)
    hot = slot_ref[...] == lax.broadcasted_iota(jnp.int32, (F, F), 0)
    perm = jnp.where(hot, 1.0, 0.0).astype(BF)

    wacc[...] = jnp.zeros_like(wacc)
    gacc[...] = jnp.zeros_like(gacc)

    def pair_steps(p):
        columns = slice(p * PW, (p + 1) * PW)
        x = dot(perm, unslot(recv_ref[:, slot_rows(p)], f_dev))
        scale = scale_ref[...]
        x = (x * jnp.concatenate([scale] * PAIR, axis=1)).astype(BF)
        yield
        same = (
            lax.broadcasted_iota(jnp.int32, (PAIR * K, PW), 0) // K
            == lax.broadcasted_iota(jnp.int32, (PAIR * K, PW), 1) // E
        )
        saved = []
        for layer in range(LAYERS):
            xs[layer, :, columns] = x
            projected = dot(left_ref[layer, F:], x)
            projected = jnp.concatenate([projected] * PAIR, axis=0)
            projected = jnp.where(same, projected, 0.0).astype(BF)
            paired = dot_nt(x, projected).astype(BF)
            mixed = dot(
                jnp.concatenate([left_ref[layer, :F], paired], axis=1),
                jnp.concatenate([x, diag_ref[layer]], axis=0),
            )
            gain = gain_ref[layer : layer + 1, :]
            saved.append((x, projected, paired))
            yield
            for t in range(PAIR):
                lanes = slice(t * E, (t + 1) * E)
                for r in range(0, F, CHUNK):
                    rows = slice(r, r + CHUNK)
                    total = x[rows, lanes].astype(F32) + mixed[rows, lanes]
                    centred = total - jnp.sum(total, axis=-1, keepdims=True) * (1.0 / E)
                    variance = jnp.sum(centred * centred, axis=-1, keepdims=True) * (1.0 / E)
                    inverse = lax.rsqrt(variance + EPS)
                    normed = centred * inverse
                    normed_s[p, layer, rows, lanes] = normed
                    inv_s[p, layer, rows, lanes] = jnp.broadcast_to(inverse, (CHUNK, E))
                    out = (normed * gain).astype(BF)
                    if layer == LAYERS - 1:
                        feats_ref[p * PAIR + t, rows, :] = out
                    else:
                        next_s[p, rows, lanes] = out
            yield
            x = next_s[p]

        for layer in reversed(range(LAYERS)):
            x, projected, paired = saved[layer]
            gain = gain_ref[layer : layer + 1, :]
            dgain = jnp.zeros((8, E), F32)
            for t in range(PAIR):
                lanes = slice(t * E, (t + 1) * E)
                for r in range(0, F, CHUNK):
                    rows = slice(r, r + CHUNK)
                    if layer == LAYERS - 1:
                        upper = cot_ref[p * PAIR + t, rows, :].astype(F32)
                    else:
                        upper = next_s[p, rows, lanes].astype(F32)
                    normed = normed_s[p, layer, rows, lanes]
                    dgain = dgain + jnp.sum((upper * normed).reshape(CHUNK // 8, 8, E), axis=0)
                    scaled = upper * gain
                    first = jnp.sum(scaled, axis=-1, keepdims=True) * (1.0 / E)
                    second = jnp.sum(scaled * normed, axis=-1, keepdims=True) * (1.0 / E)
                    total = inv_s[p, layer, rows, lanes] * (scaled - first - normed * second)
                    grad_s[p, rows, lanes] = total
                    next_s[p, rows, lanes] = total.astype(BF)
            gacc[layer] += dgain
            yield
            total_low = next_s[p]
            ts[layer, :F, columns] = total_low
            grad_paired = dot_nt(total_low, diag_ref[layer]).astype(BF)
            wide = dot_tn(grad_paired, x)
            grad_projected = jnp.concatenate(
                [wide[t * K : (t + 1) * K, t * E : (t + 1) * E] for t in range(PAIR)], axis=1
            ).astype(BF)
            ts[layer, F:, columns] = grad_projected
            wide = dot_tn(paired, total_low)
            for t in range(PAIR):
                wacc[layer] += wide[t * K : (t + 1) * K, t * E : (t + 1) * E]
            rest = jnp.zeros((E - K, PW), BF)
            upstream = dot(
                jnp.concatenate([back_ref[layer], grad_paired, project_ref[layer]], axis=1),
                jnp.concatenate([total_low, projected, grad_projected, rest], axis=0),
            )
            yield
            for t in range(PAIR):
                lanes = slice(t * E, (t + 1) * E)
                for r in range(0, F, CHUNK):
                    rows = slice(r, r + CHUNK)
                    out = grad_s[p, rows, lanes] + upstream[rows, lanes]
                    out = (out * scale_ref[rows] if layer == 0 else out).astype(BF)
                    next_s[p, rows, lanes] = out

        slots = dot(held["unperm"][...], next_s[p])
        if f_dev % 16 == 0:
            slots = slots.astype(BF)
        for t in range(PAIR):
            low = (p * PAIR + t) * f_dev
            slots_ref[:, low : low + f_dev, :] = (
                slots[:, t * E : (t + 1) * E].reshape(F // f_dev, f_dev, E).astype(BF)
            )
        yield

    def weight_grads(layer):
        dm[layer] = dot_nt(ts[layer], xs[layer])
        gain_row = jnp.sum(gacc[layer], axis=0, keepdims=True)
        if not packed:
            mix_ref, project_t_ref, output_ref, gain_out_ref = grad_refs
            mix_ref[layer] = dm[layer, :F, :]
            project_t_ref[layer] = dm[layer, F:, :]
            output_ref[layer] = wacc[layer]
            gain_out_ref[layer : layer + 1, :] = gain_row
            return
        half = F // 2
        for d in range(2):
            for q in range(8):
                low = d * half + (q // 4) * E
                pj[d, layer * 8 + q] = dm[
                    layer, F + 8 * (q % 4) : F + 8 * (q % 4) + 8, low : low + E
                ]
                if q < 2:
                    low = d * (K // 2) + 8 * q
                    ex[d, layer * 8 + q] = wacc[layer, low : low + 8, :]
                else:
                    row = gain_row[:, d * 64 : (d + 1) * 64]
                    ex[d, layer * 8 + q] = jnp.broadcast_to(
                        jnp.concatenate([row, row], axis=1), (8, E)
                    )
        my_d, my_m = pos_ref[0], pos_ref[1]
        flip = (my_m >> 3) ^ layer
        for core in range(2):
            for rx in range(2):
                for ry in range(2):
                    for low_z in range(2):
                        q = (my_m & 7) ^ (low_z * 4 + rx * 2 + core)
                        d = my_d ^ ry
                        start = pl.multiple_of(d * half + q * 32, 32)
                        block = dm[layer, pl.ds(start, 32), :]
                        pieces = [block[:, c * E : (c + 1) * E] for c in range(4)]
                        pieces += [pj[d, layer * 8 + q], ex[d, layer * 8 + q]]
                        place = (rx * 2 + ry) * 4 + low_z + 2 * flip
                        grad_refs[core][place] = jnp.concatenate(pieces, axis=0).astype(BF)

    programs = [pair_steps(p) for p in range(PAIRS)]
    phases = 4 * LAYERS + 2
    for tick in range(phases):
        if tick == 0:
            copies.wait("recv", "scale")
        if tick == 1:
            copies.wait("left", "diag")
        if tick == 2 * LAYERS + 1:
            copies.wait("cot", "back", "project", "unperm")
        if tick == 2 * LAYERS + 1:
            copies.start("feats", feats_ref, feats_hbm)
        for program in programs:
            next(program)
        for layer in reversed(range(LAYERS)):
            if tick == phases - 1 - 2 * layer:
                weight_grads(layer)
    copies.start("slots", slots_ref, slots_hbm)
    for n in range(grads):
        copies.start(("grad", n), grad_refs[n], grad_outs[n])
    copies.drain()


def run_layers(pos, slot_feature, recv, cotangent, operands, f_dev, packed):
    left, back, diag, project, gain, scale, unperm = operands
    tables = F // f_dev

    def shape(dims, dtype=F32):
        return jax.ShapeDtypeStruct(dims, dtype)

    if packed:
        grads = [shape((16, PIECE, E), BF)] * 2
    else:
        grads = [
            shape((LAYERS, F, F)),
            shape((LAYERS, K, F)),
            shape((LAYERS, K, E)),
            shape((LAYERS, E)),
        ]
    given = dict(
        scale=scale, left=left, diag=diag, back=back, project=project, unperm=unperm
    )
    constants = [given[name] for name in CONSTANTS]
    width = SAMP_DEV * E
    big = [shape((SAMP_DEV, F, E), BF), shape((tables, SAMP_DEV * f_dev, E), BF)]
    outs = big + grads

    def scratch(x):
        return pltpu.VMEM(x.shape, x.dtype)

    copies = len(constants) + 4 + len(grads)
    return pl.pallas_call(
        functools.partial(layers_kernel, f_dev=f_dev, packed=packed),
        out_shape=outs,
        in_specs=[pl.BlockSpec(memory_space=pltpu.SMEM), VMEM, VMEM]
        + [HBM] * (2 + len(constants)),
        out_specs=[HBM] * len(outs),
        scratch_shapes=[scratch(x) for x in constants]
        + [scratch(recv), scratch(cotangent)]
        + [scratch(x) for x in outs]
        + [
            pltpu.VMEM((LAYERS, F, width), BF),
            pltpu.VMEM((LAYERS, F + K, width), BF),
            pltpu.VMEM((PAIRS, LAYERS, F, PW), F32),
            pltpu.VMEM((PAIRS, LAYERS, F, PW), F32),
            pltpu.VMEM((PAIRS, F, PW), F32),
            pltpu.VMEM((PAIRS, F, PW), BF),
            pltpu.VMEM((LAYERS, K, E), F32),
            pltpu.VMEM((LAYERS, 8, E), F32),
            pltpu.VMEM((LAYERS, F + K, F), F32),
            pltpu.VMEM((2, 16, 8, E), F32),
            pltpu.VMEM((2, 16, 8, E), F32),
            pltpu.SemaphoreType.DMA((copies,)),
        ],
        compiler_params=params(WHOLE),
        name="layers",
    )(pos, gain, slot_feature.reshape(1, F), recv, cotangent, *constants)


def across(x, d, m):
    pairs = [(i, i ^ (d * 16 + m)) for i in range(32)]
    return lax.ppermute(x, ("dp", "mp"), pairs)


def added(parts):
    return sum(part.astype(F32) for part in parts).astype(BF)


def finish_kernel(pos_ref, *refs, factor):
    parts = refs[:4]
    mix_ref, project_ref, output_ref, gain_ref, pj, ex = refs[4:]
    my_m = pos_ref[1]
    for c in range(2):
        for rx in range(2):
            for rz in range(4):
                m = my_m ^ (rz * 4 + rx * 2 + c)
                piece = parts[c * 2 + rx][rz].astype(F32) * factor
                start = pl.multiple_of((m & 7) * 32, 32)
                for n in range(4):
                    mix_ref[m >> 3, pl.ds(start, 32), n * E : (n + 1) * E] = piece[
                        n * 32 : (n + 1) * 32
                    ]
                pj[m] = piece[128:136]
                ex[m] = piece[136:144]
    for l in range(LAYERS):
        for h in range(2):
            for b in range(4):
                project_ref[l, b * 8 : (b + 1) * 8, h * E : (h + 1) * E] = pj[l * 8 + h * 4 + b]
        for b in range(2):
            output_ref[l, b * 8 : (b + 1) * 8, :] = ex[l * 8 + b]
        gain_ref[l : l + 1, :] = ex[l * 8 + 2][0:1, :64]


def finish(pos, parts, factor):
    return pl.pallas_call(
        functools.partial(finish_kernel, factor=factor),
        out_shape=[
            jax.ShapeDtypeStruct((LAYERS, F // 2, F), F32),
            jax.ShapeDtypeStruct((LAYERS, K, F // 2), F32),
            jax.ShapeDtypeStruct((LAYERS, K // 2, E), F32),
            jax.ShapeDtypeStruct((LAYERS, E // 2), F32),
        ],
        in_specs=[pl.BlockSpec(memory_space=pltpu.SMEM)] + [VMEM] * 4,
        out_specs=[VMEM] * 4,
        scratch_shapes=[pltpu.VMEM((16, 8, E), F32)] * 2,
        compiler_params=params(PART),
        name="finish",
    )(pos, *parts)


def exchange(x):
    return lax.all_to_all(x, "mp", split_axis=0, concat_axis=0, tiled=True)


def return_packed(pos, slots, keep, send, ids, factor):
    rows, bags = ids.shape[1], slots.shape[0] * slots.shape[1]
    other = across(send, 0, 1)
    both = [part.reshape(2, 2, 4, PIECE, E) for part in (keep, other)]
    to_y, own = (added([part[:, ry] for part in both]) for ry in (1, 0))
    both = [own, across(to_y, 1, 0)]
    to_x, own = (added([part[rx] for part in both]) for rx in (1, 0))
    parts = [own, across(to_x, 0, 2)]
    owner = exchange(slots)
    both = [part.reshape(2, 2, PIECE, E) for part in parts]
    to_near, own = (added([part[:, near] for part in both]) for near in (1, 0))
    both = [own, across(to_near, 0, 4)]
    to_far, own = (added([part[far : far + 1] for part in both]) for far in (1, 0))
    piece = added([own, across(to_far, 0, 8)])
    column = jnp.concatenate([piece] + [across(piece, 0, 4 * r) for r in range(1, 4)], axis=0)
    column, owner = lax.optimization_barrier((column, owner))
    beside = across(column, 0, 2)
    row_grads = expand(ids, owner.reshape(bags, E), rows)
    beside, row_grads = lax.optimization_barrier((beside, row_grads))
    parts = [column, beside, across(column, 0, 1), across(beside, 0, 1)]
    parts, row_grads = lax.optimization_barrier((parts, row_grads))
    return row_grads, finish(pos, parts, factor)


def per_device(
    table_rows,
    bag_ids,
    slot_feature,
    block_exponent,
    fm_project,
    fm_output,
    mix_weight,
    norm_gain,
    out_cotangent,
):
    tables, groups = lax.axis_size("mp"), lax.axis_size("dp")
    f_dev = F // tables
    bags = SAMP_DEV * tables * f_dev
    rows = table_rows.shape[2]
    ids = bag_ids.reshape(1, rows)
    factor = 1.0 / float(SAMP_DEV * tables * groups) ** 0.5
    pos = jnp.stack([lax.axis_index("dp"), lax.axis_index("mp")]).astype(jnp.int32)

    pooled = pool(ids, table_rows.reshape(rows, E), bags).reshape(tables, SAMP_DEV * f_dev, E)
    recv = exchange(pooled)
    weights = (fm_project.transpose(0, 2, 1), fm_output, mix_weight, norm_gain)
    if groups == 2:
        weights = [(part, lax.ppermute(part, "dp", [(0, 1), (1, 0)])) for part in weights]
    else:
        weights = [
            (lax.all_gather(part, "dp", axis=axis, tiled=True),)
            for part, axis in zip(weights, (2, 1, 1, 1))
        ]
    operands = prepare(pos, slot_feature, block_exponent, weights)
    packed = (groups, tables) == (2, 16)
    feats, slots, *grads = run_layers(pos, slot_feature, recv, out_cotangent, operands, f_dev, packed)
    if packed:
        row_grads, shares = return_packed(pos, slots, *grads, ids, factor)
        project_t, output_g, mix_g, gain_g = shares[1], shares[2], shares[0], shares[3]
    else:
        row_grads = expand(ids, exchange(slots).reshape(bags, E), rows)
        mix_g, project_t, output_g, gain_g = (
            lax.psum_scatter(part.astype(BF), "dp", scatter_dimension=axis, tiled=True).astype(F32)
            * factor
            for part, axis in zip(lax.psum(tuple(grads), "mp"), (1, 2, 1, 1))
        )
    return (
        feats,
        row_grads.reshape(1, 1, rows, E),
        project_t.transpose(0, 2, 1),
        output_g,
        mix_g,
        gain_g,
    )


def solution(mesh):
    placed = (
        P("dp", "mp", None, None),
        P("dp", "mp", None),
        P(),
        P(),
        P(None, "dp", None),
        P(None, "dp", None),
        P(None, "dp", None),
        P(None, "dp"),
        P(("dp", "mp"), None, None),
    )
    return jax.shard_map(
        per_device,
        mesh=mesh,
        in_specs=placed,
        out_specs=(
            P(("dp", "mp"), None, None),
            P("dp", "mp", None, None),
            P(None, "dp", None),
            P(None, "dp", None),
            P(None, "dp", None),
            P(None, "dp"),
        ),
        check_vma=False,
    )
```
